256 devices in a mesh: replica: 16 (over y, x_hi, core), tensor: 8 (over z), fsdp: 2 (over x_lo).
Axes of the slice: x: 4 (x_hi: 2, x_lo: 2; x = x_hi * 2 + x_lo), y: 4, z: 8, core: 2. Of those that a mesh axis runs over, the one named last changes fastest.
Arguments:
- tokens: bfloat16 [32768, 8192], P(('replica', 'fsdp'), 'tensor'), may hold values from -600 to 600
- gain: float32 [8192], P('tensor'), may hold values from 0.1 to 1.9
- kv_weight: bfloat16 [16, 8192, 2048], P('replica', 'tensor', 'fsdp'), may hold values from -0.0625 to 0.0625
- local_params: float32 [16, 768, 8192], P('replica', ('tensor', 'fsdp')), may hold values from -70 to 70
- base_params: float32 [768, 8192], P(('tensor', 'fsdp')), may hold values from -6 to 6
- momentum: float32 [768, 8192], P(('tensor', 'fsdp')), may hold values from -6 to 6
Outputs:
- kv_heads: bfloat16 [32768, 2048], P(('replica', 'fsdp'), 'tensor')
- new_base: float32 [768, 8192], P(('tensor', 'fsdp'))
- new_momentum: float32 [768, 8192], P(('tensor', 'fsdp'))
The draws below stay inside these ranges and needn't reach their ends.
All inputs are finite; a program needn't handle non-finite values.
Results may differ from the reference program's by a relative error of at most 0.017.
Values may be sent and summed in bfloat16 or wider, within the bound.
A program may use at most 64 MiB of HBM per device.

```python
import math
import jax
import jax.numpy as jnp
from jax import lax

D = 8192
G = 128
KV = 2048
REPLICAS = 16
TOK_REP = 2048
TOKENS = 32768
FEAT = 1024
FR = 768
N_TENSOR = 8


def base_field(key):
    return jnp.clip(jax.random.normal(key, (FR, D), jnp.float32), -6.0, 6.0)


def draw_base_params(key, part):
    field = base_field(key)
    return field


def draw_local_params(key, part):
    field = base_field(key)
    key = jax.random.fold_in(key, 5)
    key_own = jax.random.fold_in(key, 0)
    key_rows = jax.random.fold_in(key, 2)
    key_cols = jax.random.fold_in(key, 3)
    noise = jnp.clip(jax.random.normal(key_own, (REPLICAS, FR, D), jnp.float32), -5.0, 5.0)
    row_scale = jnp.exp(jax.random.uniform(key_rows, (1, FR, 1), jnp.float32, math.log(0.3), math.log(3.0)))
    col_scale = jnp.exp(jax.random.uniform(key_cols, (1, 1, D), jnp.float32, math.log(0.3), math.log(3.0)))
    return field[None, :, :] - noise * row_scale * col_scale


def draw_tokens(key, part):
    key = jax.random.fold_in(key, 9)
    key_vals, key_rows, key_cols = jax.random.split(key, 3)
    position = jnp.arange(D, dtype=jnp.float32) / D
    values = jnp.clip(jax.random.normal(key_vals, (TOKENS, D), jnp.float32), -4.0, 4.0)
    row_scale = jnp.exp(jax.random.uniform(key_rows, (TOKENS, 1), jnp.float32, 0.0, math.log(10.0)))
    rising = jnp.exp(math.log(10.0) * position)
    rough = jnp.exp(jax.random.uniform(key_cols, (1, D), jnp.float32, math.log(0.7), math.log(1.4)))
    return (values * row_scale * rough * rising[None, :]).astype(jnp.bfloat16)


def block_levels(key, shape, pieces, smallest, top_value):
    factor_of = 1.0
    for axis_at, shards_of in pieces:
        draws = jax.random.uniform(jax.random.fold_in(jax.random.fold_in(key, 6), axis_at), (shards_of,), jnp.float32, smallest / len(pieces), top_value / len(pieces))
        factor_of = factor_of * jnp.repeat(jnp.exp(draws), shape[axis_at] // shards_of).reshape((-1,) + (1,) * (len(shape) - 1 - axis_at))
    return factor_of


def normal_values(stream_key, extent, spread, reach, cuts=(), kind=jnp.bfloat16):
    array = spread * jax.random.normal(stream_key, extent, jnp.float32)
    if cuts:
        array = array * block_levels(stream_key, extent, cuts, -0.22, 0.18)
    return jnp.clip(array, -reach, reach).astype(kind)


def setup_inputs(seed: int = 0) -> dict:
    seeds = jax.random.split(jax.random.key(seed), 7)
    tokens = draw_tokens(jax.random.fold_in(seeds[6], 71), 0)
    gain = jnp.clip(1.0 + 0.18 * jax.random.normal(seeds[1], (D,), jnp.float32), 0.1, 1.9)
    kv_weight = normal_values(seeds[2], (REPLICAS, D, KV), D ** -0.5, 0.0625, ((0, 16), (1, 8), (2, 2)))
    local_params = draw_local_params(jax.random.fold_in(seeds[6], 71), 0)
    base_params = draw_base_params(jax.random.fold_in(seeds[6], 71), 0)
    momentum = normal_values(seeds[5], (FR, D), 1.0, 6.0, ((0, 16),), jnp.float32)
    return dict(tokens=tokens, gain=gain, kv_weight=kv_weight, local_params=local_params, base_params=base_params, momentum=momentum)


outer_momentum = 0.9
outer_rate = 0.7
norm_eps = 1e-05
scale_eps = 1e-06

def quantize(pseudo_grad):
    blocks = pseudo_grad.reshape(FR, D // G, G)
    scales = lax.optimization_barrier((lax.optimization_barrier(jnp.max(jnp.abs(blocks), axis=2)) + scale_eps).astype(jnp.bfloat16))
    scale_wide = scales.astype(jnp.float32)[:, :, None]
    levels = lax.optimization_barrier((blocks / scale_wide).astype(jnp.bfloat16))
    return (levels.astype(jnp.float32) * scale_wide).reshape(FR, D)

def reference(tokens, gain, kv_weight, local_params, base_params, momentum):
    features = tokens.astype(jnp.float32)
    mean_square = lax.optimization_barrier(jnp.mean(features * features, axis=1, keepdims=True))
    normed = (features * lax.rsqrt(mean_square + norm_eps) * gain[None, :]).astype(jnp.bfloat16)
    grouped = normed.reshape(REPLICAS, TOK_REP, N_TENSOR, FEAT)

    def project(pair):
        rows_in, weight = pair
        terms = jnp.einsum('tnd,ndk->ntk', rows_in.astype(jnp.float32), weight.reshape(N_TENSOR, FEAT, KV).astype(jnp.float32))
        rounded = lax.optimization_barrier(terms.astype(jnp.bfloat16))
        return lax.optimization_barrier(jnp.sum(rounded.astype(jnp.float32), axis=0))
    kv_heads = lax.map(project, (grouped, kv_weight)).reshape(TOKENS, KV).astype(jnp.bfloat16)

    def accumulate(running, replica_local):
        return (running + quantize(base_params - replica_local), None)
    running, unused = lax.scan(accumulate, jnp.zeros((FR, D), jnp.float32), local_params)
    average = running / REPLICAS
    new_momentum = outer_momentum * momentum + average
    new_base = base_params - outer_rate * (average + outer_momentum * new_momentum)
    return (kv_heads, new_base, new_momentum)
```

```python
import jax
import jax.numpy as jnp
from jax import lax
from jax.experimental import pallas as pl
from jax.experimental.pallas import tpu as pltpu
from jax.sharding import PartitionSpec as P

F32 = jnp.float32
BF16 = jnp.bfloat16
MESH = pl.DeviceIdType.MESH

G = 128
OUTER_MOMENTUM = 0.9
OUTER_RATE = 0.7
NORM_EPS = 1e-05
SCALE_EPS = 1e-06
REPLICAS = 16
WIDTH = 8192
RING = 8
TOK = 1024
FEAT = 1024
COLS = 48
HALF = TOK // 2
FROWS = 48
FCOLS = 1024

ORDER = (
    (1, 0, 3, 2, 40, 51, 8, 41, 28, 29, 42, 9, 26, 43, 27, 36, 10, 24, 37, 48, 25, 38, 11, 39, 20, 32, 49, 33, 12, 22, 34, 23, 13, 46, 47, 21, 35, 14, 50, 18, 15, 19, 16, 17),
    (0, 1, 3, 2, 51, 8, 46, 47, 36, 9, 28, 29, 37, 38, 10, 18, 24, 39, 48, 19, 32, 11, 26, 33, 27, 49, 34, 12, 25, 35, 16, 40, 13, 17, 41, 42, 14, 22, 23, 43, 50, 15, 20, 21),
    (3, 2, 0, 1, 51, 8, 28, 29, 22, 9, 46, 47, 23, 20, 10, 32, 42, 21, 48, 33, 18, 11, 40, 19, 41, 49, 16, 12, 43, 17, 34, 26, 13, 35, 27, 24, 14, 36, 37, 25, 50, 15, 38, 39),
    (2, 3, 0, 1, 26, 51, 8, 27, 46, 47, 24, 9, 40, 25, 41, 22, 10, 42, 23, 48, 43, 20, 11, 21, 38, 18, 49, 19, 12, 36, 16, 37, 13, 28, 29, 39, 17, 14, 50, 32, 15, 33, 34, 35),
    (1, 3, 0, 2, 28, 46, 29, 47, 8, 51, 40, 26, 27, 41, 9, 24, 42, 25, 43, 10, 22, 36, 48, 23, 37, 11, 20, 38, 49, 16, 39, 12, 17, 34, 21, 13, 32, 18, 33, 19, 14, 35, 50, 15),
    (0, 3, 2, 1, 28, 40, 29, 41, 8, 51, 46, 26, 27, 42, 9, 22, 43, 24, 47, 10, 20, 48, 38, 21, 11, 39, 25, 32, 49, 23, 12, 33, 16, 34, 17, 13, 35, 36, 37, 14, 18, 50, 19, 15),
    (3, 0, 1, 2, 46, 26, 47, 27, 8, 51, 28, 40, 41, 24, 9, 36, 25, 42, 29, 10, 38, 48, 20, 39, 11, 21, 43, 18, 49, 37, 12, 19, 34, 16, 35, 13, 17, 22, 23, 14, 32, 50, 33, 15),
    (2, 0, 3, 1, 46, 28, 47, 29, 8, 51, 26, 40, 41, 27, 9, 42, 24, 43, 25, 10, 36, 22, 48, 37, 23, 11, 38, 20, 49, 34, 21, 12, 35, 16, 39, 13, 18, 32, 19, 33, 14, 17, 50, 15),
)
ARRIVAL = (
    (8, 11, 10, 12, 13, 9, 15, 14),
    (11, 10, 12, 13, 8, 9, 15, 14),
    (12, 13, 11, 10, 15, 14, 8, 9),
    (15, 12, 13, 11, 10, 14, 8, 9),
    (14, 15, 12, 13, 11, 10, 9, 8),
    (15, 8, 12, 9, 13, 14, 11, 10),
    (8, 15, 11, 14, 10, 9, 12, 13),
    (9, 8, 11, 10, 12, 13, 14, 15),
)


def pick(values, place):
    value = jnp.int32(values[0])
    for c in range(1, RING):
        value = jnp.where(place == c, jnp.int32(values[c]), value)
    return value


def packed(codes, bits):
    return sum(code << (bits * i) for i, code in enumerate(codes))


def kernel(
    tokens, gain, weight, local, base, momentum,
    out, out_base, out_mom,
    tok, xg, gvec, wl, wr, prod, sbuf, rbuf, sq, sqr, rsf, outv,
    bv, lv, mv, vbuf, frecv, fsum, xr, fown, fall,
    load_sem, store_sem, xs, xrs, zs, zr, qs, qr, fs, fr, hs, hr, gs, gr,
):
    rep = lax.axis_index("replica")
    t = lax.axis_index("tensor")
    f = lax.axis_index("fsdp")
    place = lax.rem(t + 4 * f, RING)
    other = lax.rem(place + 4, RING)
    y = rep // 4
    xh = lax.rem(rep // 2, 2)
    core = lax.rem(rep, 2)
    k = y * 2 + core

    def member(delta):
        p = lax.rem(k + delta, RING)
        return p, ((p // 2) * 4 + xh * 2 + lax.rem(p, 2), t, f)

    def on_ring(delta):
        return (rep, lax.rem(t + delta, RING), f)

    x_dev = (rep, t, 1 - f)
    h_dev = (y * 4 + (1 - xh) * 2 + core, t, f)

    loads = []
    for i, (src, dst) in enumerate(
        ((tokens, tok), (gain, gvec), (weight.at[0], wl), (base, bv), (local.at[0], lv), (momentum, mv))
    ):
        loads.append(pltpu.make_async_copy(src, dst, load_sem.at[i]))
        loads[-1].start()

    barrier = pltpu.get_barrier_semaphore()
    pl.semaphore_signal(barrier, inc=1, device_id=x_dev, device_id_type=MESH)
    pl.semaphore_signal(barrier, inc=1, device_id=h_dev, device_id_type=MESH)
    for delta in range(1, RING):
        pl.semaphore_signal(barrier, inc=1, device_id=on_ring(delta), device_id_type=MESH)
        pl.semaphore_signal(barrier, inc=1, device_id=member(delta)[1], device_id_type=MESH)
    pl.semaphore_wait(barrier, 2 + 2 * (RING - 1))

    x_copies = []
    for j in range(8):
        part = pick([row[j] - 8 for row in ARRIVAL], other)
        x_copies.append(
            pltpu.make_async_remote_copy(
                src_ref=weight.at[0, :, pl.ds(pl.multiple_of(part * 128, 128), 128)],
                dst_ref=wr.at[j],
                send_sem=xs.at[j],
                recv_sem=xrs.at[j],
                device_id=x_dev,
                device_id_type=MESH,
            )
        )
        x_copies[-1].start()

    words = [
        pick([packed(row[n : n + 5], 6) for row in ORDER], place) for n in range(0, len(ORDER[0]), 5)
    ]
    arrival = pick([packed([u - 8 for u in row], 3) for row in ARRIVAL], place)

    loads[0].wait()
    loads[1].wait()

    @pl.loop(0, TOK // 128)
    def _(i):
        rows = pl.ds(pl.multiple_of(i * 128, 128), 128)
        xg[rows, :] = (tok[rows, :].astype(F32) * gvec[...]).astype(BF16)

    loads[2].wait()

    def sq_copy(delta):
        return pltpu.make_async_remote_copy(
            src_ref=sq, dst_ref=sqr.at[delta - 1], send_sem=qs.at[delta - 1], recv_sem=qr.at[delta - 1],
            device_id=on_ring(delta), device_id_type=MESH,
        )

    def rs_copy(delta):
        p, dev = member(delta)
        return pltpu.make_async_remote_copy(
            src_ref=vbuf.at[p], dst_ref=frecv.at[delta - 1], send_sem=fs.at[delta - 1],
            recv_sem=fr.at[delta - 1], device_id=dev, device_id_type=MESH,
        )

    def h_copy():
        return pltpu.make_async_remote_copy(
            src_ref=fsum, dst_ref=xr, send_sem=hs.at[0], recv_sem=hr.at[0], device_id=h_dev, device_id_type=MESH
        )

    def ag_copy(delta):
        return pltpu.make_async_remote_copy(
            src_ref=fown, dst_ref=fall.at[delta - 1], send_sem=gs.at[delta - 1], recv_sem=gr.at[delta - 1],
            device_id=member(delta)[1], device_id_type=MESH,
        )

    def z_copy(idx, h, dev):
        return pltpu.make_async_remote_copy(
            src_ref=sbuf.at[idx, h], dst_ref=rbuf.at[idx, h], send_sem=zs.at[idx * 2 + h],
            recv_sem=zr.at[idx * 2 + h], device_id=dev, device_id_type=MESH,
        )

    def own_product(q):
        cols = pl.ds(pl.multiple_of(q * 256, 256), 256)

        @pl.loop(0, TOK // 256)
        def _(i):
            rows = pl.ds(pl.multiple_of(i * 256, 256), 256)
            res = jnp.dot(xg[rows, :], wl[:, cols], preferred_element_type=F32)
            part = pl.ds(pl.multiple_of(lax.rem(i, 2) * 256, 256), 256)
            prod[2 * q, i // 2, part, :] = res[:, :128]
            prod[2 * q + 1, i // 2, part, :] = res[:, 128:]

    def other_product(j):
        pltpu.make_async_remote_copy(
            src_ref=wr.at[j], dst_ref=wr.at[j], send_sem=xs.at[j], recv_sem=xrs.at[j],
            device_id=x_dev, device_id_type=MESH,
        ).wait_recv()
        u = 8 + lax.bitwise_and(lax.shift_right_logical(arrival, 3 * j), jnp.int32(7))

        @pl.loop(0, TOK // 256)
        def _(i):
            rows = pl.ds(pl.multiple_of(i * 256, 256), 256)
            part = pl.ds(pl.multiple_of(lax.rem(i, 2) * 256, 256), 256)
            prod[u, i // 2, part, :] = jnp.dot(xg[rows, :], wr[j], preferred_element_type=F32)

    def pass_on(code):
        h = lax.rem(code, 2)
        idx = code // 2
        up = idx // 8
        r = lax.rem(idx, 8) // 2 + 1
        s = lax.rem(idx, 2)
        step = 2 * up - 1
        u = 2 * lax.rem(place + step * r + RING, RING) + s
        dev = on_ring(step + RING)
        first = (r == 4) | ((r == 3) & (s == 1 - up))

        @pl.when(first)
        def _():
            @pl.loop(0, HALF // 128)
            def _(i):
                rows = pl.ds(pl.multiple_of(i * 128, 128), 128)
                sbuf[idx, h, rows, :] = prod[u, h, rows, :].astype(BF16)

        @pl.when(jnp.logical_not(first))
        def _():
            z_copy(idx + 2, h, dev).wait_recv()

            @pl.loop(0, HALF // 128)
            def _(i):
                rows = pl.ds(pl.multiple_of(i * 128, 128), 128)
                sbuf[idx, h, rows, :] = (
                    prod[u, h, rows, :] + rbuf[idx + 2, h, rows, :].astype(F32)
                ).astype(BF16)

        z_copy(idx, h, dev).start()

    def fragment_start():
        ones = jnp.ones((16, FEAT), BF16)
        sub = lax.broadcasted_iota(jnp.int32, (8, 128), 0)
        acc = jnp.zeros((8, 128), F32)
        for i in range(TOK // 256):
            x = tok[i * 256 : (i + 1) * 256, :].astype(F32)
            x2 = x * x
            hi = x2.astype(BF16)
            lo = (x2 - hi.astype(F32)).astype(BF16)
            dims = (((1,), (1,)), ((), ()))
            row = lax.dot_general(ones, hi, dims, preferred_element_type=F32)
            row = row + lax.dot_general(ones, lo, dims, preferred_element_type=F32)
            for g in range(2):
                acc = acc + jnp.where(sub == 2 * i + g, row[0:8, g * 128 : (g + 1) * 128], 0.0)
        sq[...] = acc
        for delta in range(1, RING):
            sq_copy(delta).start()

        loads[3].wait()
        loads[4].wait()

        @pl.loop(0, RING)
        def _(p):
            for g in range(FCOLS // G):
                cols = pl.ds(pl.multiple_of(p * FCOLS + g * G, G), G)
                grad = bv[:, cols] - lv[:, cols]
                top = jnp.max(jnp.abs(grad), axis=1, keepdims=True)
                scale = (top + SCALE_EPS).astype(BF16).astype(F32)
                level = (grad / scale).astype(BF16).astype(F32)
                vbuf[p, :, g * G : (g + 1) * G] = (level * scale).astype(BF16)

        for delta in range(1, RING):
            rs_copy(delta).start()

    def fragment_sum():
        for delta in range(1, RING):
            rs_copy(delta).wait_recv()
        total = vbuf[k].astype(F32)
        for delta in range(1, RING):
            total = total + frecv[delta - 1].astype(F32)
        fsum[...] = total.astype(BF16)
        h_copy().start()

    def fragment_spread():
        h_copy().wait_recv()
        fown[...] = (fsum[...].astype(F32) + xr[...].astype(F32)).astype(BF16)
        for delta in range(1, RING):
            ag_copy(delta).start()

    stores = [
        pltpu.make_async_copy(bv, out_base, store_sem.at[0]),
        pltpu.make_async_copy(mv, out_mom, store_sem.at[1]),
    ]

    def fragment_end():
        for delta in range(1, RING):
            ag_copy(delta).wait_recv()
        loads[5].wait()

        for delta in range(RING):
            p = lax.rem(k + RING - delta, RING)
            cols = pl.ds(pl.multiple_of(p * FCOLS, FCOLS), FCOLS)
            piece = fown[...] if delta == 0 else fall[delta - 1]
            average = piece.astype(F32) / REPLICAS
            new_mom = OUTER_MOMENTUM * mv[:, cols] + average
            mv[:, cols] = new_mom
            bv[:, cols] = bv[:, cols] - OUTER_RATE * (average + OUTER_MOMENTUM * new_mom)

        for store in stores:
            store.start()

        total = sq[...]
        for delta in range(1, RING):
            sq_copy(delta).wait_recv()
            total = total + sqr[delta - 1]
        rs = lax.rsqrt(total / WIDTH + NORM_EPS)
        for g in range(TOK // 128):
            rsf[g // 4, g % 4 * 128 : (g % 4 + 1) * 128, :] = jnp.broadcast_to(rs[g : g + 1, :], (128, 128)).T

    @pl.loop(0, len(ORDER[0]))
    def _(n):
        word = words[0]
        for i in range(1, len(words)):
            word = jnp.where(n // 5 == i, words[i], word)
        code = lax.bitwise_and(lax.shift_right_logical(word, 6 * lax.rem(n, 5)), jnp.int32(63))

        @pl.when(code < 8)
        def _():
            own_product(code)

        @pl.when((code >= 8) & (code < 16))
        def _():
            other_product(code - 8)

        @pl.when((code >= 16) & (code < 48))
        def _():
            pass_on(code - 16)

        @pl.when(code == 51)
        def _():
            fragment_start()

        @pl.when(code == 48)
        def _():
            fragment_sum()

        @pl.when(code == 49)
        def _():
            fragment_spread()

        @pl.when(code == 50)
        def _():
            fragment_end()

    for h in range(2):
        for s in range(2):
            z_copy(s, h, on_ring(1)).wait_recv()
            z_copy(8 + s, h, on_ring(1)).wait_recv()

            @pl.loop(0, HALF // 128)
            def _(i):
                rows = pl.ds(pl.multiple_of(i * 128, 128), 128)
                total = prod[2 * place + s, h, rows, :] + rbuf[s, h, rows, :].astype(F32)
                total = total + rbuf[8 + s, h, rows, :].astype(F32)
                outv[h, rows, s * 128 : (s + 1) * 128] = (total * rsf[h, rows, :]).astype(BF16)

        stores.append(
            pltpu.make_async_copy(
                outv.at[h], out.at[pl.ds(h * HALF, HALF)], store_sem.at[2 + h]
            )
        )
        stores[-1].start()

    for copy in x_copies:
        copy.wait_send()
    for idx in range(16):
        if idx in (6 + 1, 8 + 6):
            continue
        for h in range(2):
            z_copy(idx, h, on_ring(1)).wait_send()
    for delta in range(1, RING):
        sq_copy(delta).wait_send()
        rs_copy(delta).wait_send()
        ag_copy(delta).wait_send()
    h_copy().wait_send()
    for store in stores:
        store.wait()


def body(tokens, gain, weight, local, base, momentum):
    dma = pltpu.SemaphoreType.DMA
    any_spec = pl.BlockSpec(memory_space=pl.ANY)
    return pl.pallas_call(
        kernel,
        out_shape=(
            jax.ShapeDtypeStruct((TOK, 256), BF16),
            jax.ShapeDtypeStruct(base.shape, F32),
            jax.ShapeDtypeStruct(base.shape, F32),
        ),
        in_specs=[any_spec] * 6,
        out_specs=[any_spec] * 3,
        scratch_shapes=[
            pltpu.VMEM((TOK, FEAT), BF16),
            pltpu.VMEM((TOK, FEAT), BF16),
            pltpu.VMEM((1, FEAT), F32),
            pltpu.VMEM((FEAT, 1024), BF16),
            pltpu.VMEM((8, FEAT, 128), BF16),
            pltpu.VMEM((16, 2, HALF, 128), F32),
            pltpu.VMEM((16, 2, HALF, 128), BF16),
            pltpu.VMEM((16, 2, HALF, 128), BF16),
            pltpu.VMEM((8, 128), F32),
            pltpu.VMEM((RING - 1, 8, 128), F32),
            pltpu.VMEM((2, HALF, 128), F32),
            pltpu.VMEM((2, HALF, 256), BF16),
            pltpu.VMEM((FROWS, WIDTH), F32),
            pltpu.VMEM((FROWS, WIDTH), F32),
            pltpu.VMEM((FROWS, WIDTH), F32),
            pltpu.VMEM((RING, FROWS, FCOLS), BF16),
            pltpu.VMEM((RING - 1, FROWS, FCOLS), BF16),
            pltpu.VMEM((FROWS, FCOLS), BF16),
            pltpu.VMEM((FROWS, FCOLS), BF16),
            pltpu.VMEM((FROWS, FCOLS), BF16),
            pltpu.VMEM((RING - 1, FROWS, FCOLS), BF16),
            dma((6,)),
            dma((4,)),
            dma((8,)),
            dma((8,)),
            dma((32,)),
            dma((32,)),
            dma((RING - 1,)),
            dma((RING - 1,)),
            dma((RING - 1,)),
            dma((RING - 1,)),
            dma((1,)),
            dma((1,)),
            dma((RING - 1,)),
            dma((RING - 1,)),
        ],
        compiler_params=pltpu.CompilerParams(
            collective_id=0, has_side_effects=True, vmem_limit_bytes=50 * 1024 * 1024
        ),
    )(tokens, gain.reshape(1, FEAT), weight, local, base, momentum)


def solution(mesh):
    placed = (
        P(("replica", "fsdp"), "tensor"),
        P("tensor"),
        P("replica", "tensor", "fsdp"),
        P("replica", ("tensor", "fsdp"), None),
        P(("tensor", "fsdp"), None),
        P(("tensor", "fsdp"), None),
    )
    return jax.shard_map(
        body,
        mesh=mesh,
        in_specs=placed,
        out_specs=(
            P(("replica", "fsdp"), "tensor"),
            P(("tensor", "fsdp"), None),
            P(("tensor", "fsdp"), None),
        ),
        check_vma=False,
    )
```

```python
import jax
import jax.numpy as jnp
from jax import lax
from jax.experimental import pallas as pl
from jax.experimental.pallas import tpu as pltpu
from jax.sharding import PartitionSpec as P

F32 = jnp.float32
BF16 = jnp.bfloat16
MESH = pl.DeviceIdType.MESH

G = 128
OUTER_MOMENTUM = 0.9
OUTER_RATE = 0.7
NORM_EPS = 1e-05
SCALE_EPS = 1e-06
REPLICAS = 16
WIDTH = 8192
RING = 8
TOK = 1024
FEAT = 1024
COLS = 48
CUT = 4
PART = TOK // CUT
FROWS = 48
FCOLS = 1024

ORDER = (
    (
        2, 1, 0, 3, 8, 64, 65, 4, 66, 40, 41, 67, 42, 68, 9, 69, 43, 56, 57, 32, 5, 70, 33, 10,
        71, 36, 34, 60, 37, 61, 35, 58, 38, 11, 52, 39, 59, 53, 24, 62, 6, 25, 54, 26, 55, 27, 12, 63,
        48, 28, 49, 13, 76, 77, 29, 30, 78, 31, 79, 7, 14, 20, 21, 50, 22, 23, 51, 15, 16, 17, 18, 19,
    ),
    (
        2, 0, 3, 1, 8, 76, 77, 4, 78, 79, 56, 9, 57, 40, 41, 58, 42, 59, 43, 5, 20, 60, 10, 21,
        61, 48, 22, 49, 23, 62, 32, 11, 63, 33, 52, 34, 53, 35, 50, 16, 6, 64, 17, 51, 18, 12, 36, 54,
        65, 37, 66, 38, 67, 39, 13, 28, 55, 29, 30, 31, 7, 14, 68, 69, 19, 70, 71, 15, 24, 25, 26, 27,
    ),
    (
        1, 3, 0, 2, 8, 40, 41, 4, 42, 43, 28, 9, 29, 76, 77, 30, 78, 31, 79, 5, 48, 24, 10, 49,
        25, 20, 50, 21, 51, 26, 68, 11, 27, 69, 16, 70, 17, 71, 22, 52, 6, 36, 53, 23, 54, 12, 64, 18,
        37, 65, 38, 66, 39, 67, 13, 56, 19, 57, 58, 59, 7, 14, 32, 33, 55, 34, 35, 15, 60, 61, 62, 63,
    ),
    (
        1, 2, 3, 0, 8, 36, 37, 4, 38, 76, 77, 39, 78, 32, 9, 33, 79, 28, 29, 68, 5, 34, 69, 10,
        35, 64, 70, 24, 65, 25, 71, 30, 66, 11, 16, 67, 31, 17, 60, 26, 6, 61, 18, 62, 19, 63, 12, 27,
        20, 56, 21, 13, 40, 41, 57, 58, 42, 59, 43, 7, 14, 48, 49, 22, 50, 51, 23, 15, 52, 53, 54, 55,
    ),
    (
        3, 0, 40, 41, 2, 42, 1, 8, 43, 64, 65, 36, 4, 66, 37, 67, 32, 9, 33, 76, 77, 34, 78, 35,
        79, 38, 5, 10, 39, 60, 24, 61, 25, 56, 20, 62, 11, 68, 69, 26, 27, 70, 71, 6, 21, 57, 22, 58,
        23, 59, 12, 28, 52, 29, 53, 16, 54, 30, 55, 13, 17, 63, 18, 48, 19, 49, 7, 14, 50, 51, 31, 15,
    ),
    (
        3, 1, 2, 0, 8, 40, 41, 76, 77, 4, 42, 78, 43, 79, 32, 64, 9, 33, 56, 34, 57, 35, 58, 5,
        59, 28, 10, 20, 65, 21, 66, 22, 67, 23, 52, 11, 29, 53, 30, 68, 31, 54, 36, 6, 69, 37, 70, 24,
        71, 12, 38, 60, 25, 61, 26, 62, 27, 63, 13, 39, 48, 49, 50, 7, 14, 55, 16, 17, 51, 18, 19, 15,
    ),
    (
        0, 2, 1, 3, 8, 76, 77, 40, 41, 4, 78, 42, 79, 43, 68, 36, 9, 69, 28, 70, 29, 71, 30, 5,
        31, 56, 10, 48, 37, 49, 38, 50, 39, 51, 16, 11, 57, 17, 58, 32, 59, 18, 64, 6, 33, 65, 34, 60,
        35, 12, 66, 24, 61, 25, 62, 26, 63, 27, 13, 67, 20, 21, 22, 7, 14, 19, 52, 53, 23, 54, 55, 15,
    ),
    (
        0, 3, 76, 77, 1, 78, 2, 8, 79, 36, 37, 64, 4, 38, 65, 39, 68, 9, 69, 40, 41, 70, 42, 71,
        43, 66, 5, 10, 67, 24, 60, 25, 61, 28, 48, 26, 11, 32, 33, 62, 63, 34, 35, 6, 49, 29, 50, 30,
        51, 31, 12, 56, 16, 57, 17, 52, 18, 58, 19, 13, 53, 27, 54, 20, 55, 21, 7, 14, 22, 23, 59, 15,
    ),
)
ARRIVAL = (
    (
        8, 10, 11, 12, 13, 9, 15, 14,
    ),
    (
        11, 10, 12, 8, 13, 15, 9, 14,
    ),
    (
        12, 13, 11, 15, 10, 8, 14, 9,
    ),
    (
        15, 13, 12, 11, 10, 14, 8, 9,
    ),
    (
        14, 13, 12, 15, 11, 10, 9, 8,
    ),
    (
        9, 14, 13, 12, 15, 11, 8, 10,
    ),
    (
        14, 9, 10, 11, 8, 12, 15, 13,
    ),
    (
        9, 10, 11, 8, 12, 13, 14, 15,
    ),
)


def pick(values, place):
    value = jnp.int32(values[0])
    for c in range(1, RING):
        value = jnp.where(place == c, jnp.int32(values[c]), value)
    return value


def packed(codes, bits):
    return sum(code << (bits * i) for i, code in enumerate(codes))


def kernel(
    tokens, gain, weight, local, base, momentum,
    out, out_base, out_mom,
    tok, xg, gvec, wl, wr, prod, sbuf, rbuf, sq, sqr, rsf, outv,
    bv, lv, mv, vbuf, frecv, fsum, xr, fown, fall,
    load_sem, store_sem, xs, xrs, zs, zr, qs, qr, fs, fr, hs, hr, gs, gr,
):
    rep = lax.axis_index("replica")
    t = lax.axis_index("tensor")
    f = lax.axis_index("fsdp")
    place = lax.rem(t + 4 * f, RING)
    other = lax.rem(place + 4, RING)
    y = rep // 4
    xh = lax.rem(rep // 2, 2)
    core = lax.rem(rep, 2)
    k = y * 2 + core

    def member(delta):
        p = lax.rem(k + delta, RING)
        return p, ((p // 2) * 4 + xh * 2 + lax.rem(p, 2), t, f)

    def on_ring(delta):
        return (rep, lax.rem(t + delta, RING), f)

    x_dev = (rep, t, 1 - f)
    h_dev = (y * 4 + (1 - xh) * 2 + core, t, f)

    loads = []
    for i, (src, dst) in enumerate(
        ((tokens, tok), (gain, gvec), (weight.at[0], wl), (base, bv), (local.at[0], lv), (momentum, mv))
    ):
        loads.append(pltpu.make_async_copy(src, dst, load_sem.at[i]))
        loads[-1].start()

    barrier = pltpu.get_barrier_semaphore()
    pl.semaphore_signal(barrier, inc=1, device_id=x_dev, device_id_type=MESH)
    pl.semaphore_signal(barrier, inc=1, device_id=h_dev, device_id_type=MESH)
    for delta in range(1, RING):
        pl.semaphore_signal(barrier, inc=1, device_id=on_ring(delta), device_id_type=MESH)
        pl.semaphore_signal(barrier, inc=1, device_id=member(delta)[1], device_id_type=MESH)
    pl.semaphore_wait(barrier, 2 + 2 * (RING - 1))

    x_copies = []
    for j in range(8):
        part = pick([row[j] - 8 for row in ARRIVAL], other)
        x_copies.append(
            pltpu.make_async_remote_copy(
                src_ref=weight.at[0, :, pl.ds(pl.multiple_of(part * 128, 128), 128)],
                dst_ref=wr.at[j],
                send_sem=xs.at[j],
                recv_sem=xrs.at[j],
                device_id=x_dev,
                device_id_type=MESH,
            )
        )
    for copy in x_copies[:4]:
        copy.start()

    def sq_copy(delta):
        return pltpu.make_async_remote_copy(
            src_ref=sq, dst_ref=sqr.at[delta - 1], send_sem=qs.at[delta - 1], recv_sem=qr.at[delta - 1],
            device_id=on_ring(delta), device_id_type=MESH,
        )

    def rs_copy(delta):
        p, dev = member(delta)
        return pltpu.make_async_remote_copy(
            src_ref=vbuf.at[p], dst_ref=frecv.at[delta - 1], send_sem=fs.at[delta - 1],
            recv_sem=fr.at[delta - 1], device_id=dev, device_id_type=MESH,
        )

    def h_copy():
        return pltpu.make_async_remote_copy(
            src_ref=fsum, dst_ref=xr, send_sem=hs.at[0], recv_sem=hr.at[0], device_id=h_dev, device_id_type=MESH
        )

    def ag_copy(delta):
        return pltpu.make_async_remote_copy(
            src_ref=fown, dst_ref=fall.at[delta - 1], send_sem=gs.at[delta - 1], recv_sem=gr.at[delta - 1],
            device_id=member(delta)[1], device_id_type=MESH,
        )

    def z_copy(idx, h, dev):
        return pltpu.make_async_remote_copy(
            src_ref=sbuf.at[idx, h], dst_ref=rbuf.at[idx, h], send_sem=zs.at[idx * CUT + h],
            recv_sem=zr.at[idx * CUT + h], device_id=dev, device_id_type=MESH,
        )

    loads[3].wait()
    loads[4].wait()

    @pl.loop(0, RING)
    def _(p):
        for g in range(FCOLS // G):
            cols = pl.ds(pl.multiple_of(p * FCOLS + g * G, G), G)
            grad = bv[:, cols] - lv[:, cols]
            top = jnp.max(jnp.abs(grad), axis=1, keepdims=True)
            scale = (top + SCALE_EPS).astype(BF16).astype(F32)
            level = (grad / scale).astype(BF16).astype(F32)
            vbuf[p, :, g * G : (g + 1) * G] = (level * scale).astype(BF16)

    for delta in range(1, RING):
        rs_copy(delta).start()

    words = [
        pick([packed(row[n : n + 4], 7) for row in ORDER], place) for n in range(0, len(ORDER[0]), 4)
    ]
    arrival = pick([packed([u - 8 for u in row], 3) for row in ARRIVAL], place)

    loads[0].wait()
    loads[1].wait()

    @pl.loop(0, TOK // 128)
    def _(i):
        rows = pl.ds(pl.multiple_of(i * 128, 128), 128)
        xg[rows, :] = (tok[rows, :].astype(F32) * gvec[...]).astype(BF16)

    loads[2].wait()

    def own_product(q):
        cols = pl.ds(pl.multiple_of(q * 256, 256), 256)

        res = jnp.dot(xg[...], wl[:, cols], preferred_element_type=F32)
        prod[2 * q] = res[:, :128].reshape(CUT, PART, 128)
        prod[2 * q + 1] = res[:, 128:].reshape(CUT, PART, 128)

    def other_product(j):
        pltpu.make_async_remote_copy(
            src_ref=wr.at[j], dst_ref=wr.at[j], send_sem=xs.at[j], recv_sem=xrs.at[j],
            device_id=x_dev, device_id_type=MESH,
        ).wait_recv()
        u = 8 + lax.bitwise_and(lax.shift_right_logical(arrival, 3 * j), jnp.int32(7))

        prod[u] = jnp.dot(xg[...], wr[j], preferred_element_type=F32).reshape(CUT, PART, 128)

    def pass_on(code):
        h = lax.rem(code, CUT)
        idx = code // CUT
        up = idx // 8
        r = lax.rem(idx, 8) // 2 + 1
        s = lax.rem(idx, 2)
        step = 2 * up - 1
        u = 2 * lax.rem(place + step * r + RING, RING) + s
        dev = on_ring(step + RING)
        first = (r == 4) | ((r == 3) & (s == 1 - up))

        @pl.when(first)
        def _():
            @pl.loop(0, PART // 128)
            def _(i):
                rows = pl.ds(pl.multiple_of(i * 128, 128), 128)
                sbuf[idx, h, rows, :] = prod[u, h, rows, :].astype(BF16)

        @pl.when(jnp.logical_not(first))
        def _():
            z_copy(idx + 2, h, dev).wait_recv()

            @pl.loop(0, PART // 128)
            def _(i):
                rows = pl.ds(pl.multiple_of(i * 128, 128), 128)
                sbuf[idx, h, rows, :] = (
                    prod[u, h, rows, :] + rbuf[idx + 2, h, rows, :].astype(F32)
                ).astype(BF16)

        z_copy(idx, h, dev).start()

    def squares():
        ones = jnp.ones((16, FEAT), BF16)
        sub = lax.broadcasted_iota(jnp.int32, (8, 128), 0)
        acc = jnp.zeros((8, 128), F32)
        for i in range(TOK // 256):
            x = tok[i * 256 : (i + 1) * 256, :].astype(F32)
            x2 = x * x
            hi = x2.astype(BF16)
            lo = (x2 - hi.astype(F32)).astype(BF16)
            dims = (((1,), (1,)), ((), ()))
            row = lax.dot_general(ones, hi, dims, preferred_element_type=F32)
            row = row + lax.dot_general(ones, lo, dims, preferred_element_type=F32)
            for g in range(2):
                acc = acc + jnp.where(sub == 2 * i + g, row[0:8, g * 128 : (g + 1) * 128], 0.0)
        sq[...] = acc
        for delta in range(1, RING):
            sq_copy(delta).start()

    def fragment_sum():
        for delta in range(1, RING):
            rs_copy(delta).wait_recv()
        total = vbuf[k].astype(F32)
        for delta in range(1, RING):
            total = total + frecv[delta - 1].astype(F32)
        fsum[...] = total.astype(BF16)
        h_copy().start()
        for copy in x_copies[4:]:
            copy.start()

    def fragment_spread():
        h_copy().wait_recv()
        fown[...] = (fsum[...].astype(F32) + xr[...].astype(F32)).astype(BF16)
        for delta in range(1, RING):
            ag_copy(delta).start()

    stores = [
        pltpu.make_async_copy(bv, out_base, store_sem.at[0]),
        pltpu.make_async_copy(mv, out_mom, store_sem.at[1]),
    ]

    def fragment_end():
        for delta in range(1, RING):
            ag_copy(delta).wait_recv()
        loads[5].wait()

        for delta in range(RING):
            p = lax.rem(k + RING - delta, RING)
            cols = pl.ds(pl.multiple_of(p * FCOLS, FCOLS), FCOLS)
            piece = fown[...] if delta == 0 else fall[delta - 1]
            average = piece.astype(F32) / REPLICAS
            new_mom = OUTER_MOMENTUM * mv[:, cols] + average
            mv[:, cols] = new_mom
            bv[:, cols] = bv[:, cols] - OUTER_RATE * (average + OUTER_MOMENTUM * new_mom)

        for store in stores:
            store.start()

        total = sq[...]
        for delta in range(1, RING):
            sq_copy(delta).wait_recv()
            total = total + sqr[delta - 1]
        rs = lax.rsqrt(total / WIDTH + NORM_EPS)
        for g in range(TOK // 128):
            rsf[g * 128 // PART, g * 128 % PART : g * 128 % PART + 128, :] = jnp.broadcast_to(rs[g : g + 1, :], (128, 128)).T

    @pl.loop(0, len(ORDER[0]))
    def _(n):
        word = words[0]
        for i in range(1, len(words)):
            word = jnp.where(n // 4 == i, words[i], word)
        code = lax.bitwise_and(lax.shift_right_logical(word, 7 * lax.rem(n, 4)), jnp.int32(127))

        @pl.when(code < 4)
        def _():
            own_product(code)

        @pl.when((code >= 8) & (code < 16))
        def _():
            other_product(code - 8)

        @pl.when(code >= 16)
        def _():
            pass_on(code - 16)

        @pl.when(code == 4)
        def _():
            squares()

        @pl.when(code == 5)
        def _():
            fragment_sum()

        @pl.when(code == 6)
        def _():
            fragment_spread()

        @pl.when(code == 7)
        def _():
            fragment_end()

    for h in range(CUT):
        for s in range(2):
            z_copy(s, h, on_ring(1)).wait_recv()
            z_copy(8 + s, h, on_ring(1)).wait_recv()

            @pl.loop(0, PART // 128)
            def _(i):
                rows = pl.ds(pl.multiple_of(i * 128, 128), 128)
                total = prod[2 * place + s, h, rows, :] + rbuf[s, h, rows, :].astype(F32)
                total = total + rbuf[8 + s, h, rows, :].astype(F32)
                outv[h, rows, s * 128 : (s + 1) * 128] = (total * rsf[h, rows, :]).astype(BF16)

        stores.append(
            pltpu.make_async_copy(
                outv.at[h], out.at[pl.ds(h * PART, PART)], store_sem.at[2 + h]
            )
        )
        stores[-1].start()

    for copy in x_copies:
        copy.wait_send()
    for idx in range(16):
        if idx in (6 + 1, 8 + 6):
            continue
        for h in range(CUT):
            z_copy(idx, h, on_ring(1)).wait_send()
    for delta in range(1, RING):
        sq_copy(delta).wait_send()
        rs_copy(delta).wait_send()
        ag_copy(delta).wait_send()
    h_copy().wait_send()
    for store in stores:
        store.wait()


def body(tokens, gain, weight, local, base, momentum):
    dma = pltpu.SemaphoreType.DMA
    any_spec = pl.BlockSpec(memory_space=pl.ANY)
    return pl.pallas_call(
        kernel,
        out_shape=(
            jax.ShapeDtypeStruct((TOK, 256), BF16),
            jax.ShapeDtypeStruct(base.shape, F32),
            jax.ShapeDtypeStruct(base.shape, F32),
        ),
        in_specs=[any_spec] * 6,
        out_specs=[any_spec] * 3,
        scratch_shapes=[
            pltpu.VMEM((TOK, FEAT), BF16),
            pltpu.VMEM((TOK, FEAT), BF16),
            pltpu.VMEM((1, FEAT), F32),
            pltpu.VMEM((FEAT, 1024), BF16),
            pltpu.VMEM((8, FEAT, 128), BF16),
            pltpu.VMEM((16, CUT, PART, 128), F32),
            pltpu.VMEM((16, CUT, PART, 128), BF16),
            pltpu.VMEM((16, CUT, PART, 128), BF16),
            pltpu.VMEM((8, 128), F32),
            pltpu.VMEM((RING - 1, 8, 128), F32),
            pltpu.VMEM((CUT, PART, 128), F32),
            pltpu.VMEM((CUT, PART, 256), BF16),
            pltpu.VMEM((FROWS, WIDTH), F32),
            pltpu.VMEM((FROWS, WIDTH), F32),
            pltpu.VMEM((FROWS, WIDTH), F32),
            pltpu.VMEM((RING, FROWS, FCOLS), BF16),
            pltpu.VMEM((RING - 1, FROWS, FCOLS), BF16),
            pltpu.VMEM((FROWS, FCOLS), BF16),
            pltpu.VMEM((FROWS, FCOLS), BF16),
            pltpu.VMEM((FROWS, FCOLS), BF16),
            pltpu.VMEM((RING - 1, FROWS, FCOLS), BF16),
            dma((6,)),
            dma((2 + CUT,)),
            dma((8,)),
            dma((8,)),
            dma((16 * CUT,)),
            dma((16 * CUT,)),
            dma((RING - 1,)),
            dma((RING - 1,)),
            dma((RING - 1,)),
            dma((RING - 1,)),
            dma((1,)),
            dma((1,)),
            dma((RING - 1,)),
            dma((RING - 1,)),
        ],
        compiler_params=pltpu.CompilerParams(
            collective_id=0, has_side_effects=True, vmem_limit_bytes=50 * 1024 * 1024
        ),
    )(tokens, gain.reshape(1, FEAT), weight, local, base, momentum)


def solution(mesh):
    placed = (
        P(("replica", "fsdp"), "tensor"),
        P("tensor"),
        P("replica", "tensor", "fsdp"),
        P("replica", ("tensor", "fsdp"), None),
        P(("tensor", "fsdp"), None),
        P(("tensor", "fsdp"), None),
    )
    return jax.shard_map(
        body,
        mesh=mesh,
        in_specs=placed,
        out_specs=(
            P(("replica", "fsdp"), "tensor"),
            P(("tensor", "fsdp"), None),
            P(("tensor", "fsdp"), None),
        ),
        check_vma=False,
    )
```

```python
import jax
import jax.numpy as jnp
from jax import lax
from jax.experimental import pallas as pl
from jax.experimental.pallas import tpu as pltpu
from jax.sharding import PartitionSpec as P

F32 = jnp.float32
BF16 = jnp.bfloat16
MESH = pl.DeviceIdType.MESH

G = 128
OUTER_MOMENTUM = 0.9
OUTER_RATE = 0.7
NORM_EPS = 1e-05
SCALE_EPS = 1e-06
REPLICAS = 16
WIDTH = 8192
RING = 8
FIRST = 5
TOK = 1024
FEAT = 1024
COLS = 48
CUT = 4
PART = TOK // CUT
FROWS = 48
FCOLS = 1024

ORDER = (
    (
        8, 0, 3, 2, 1, 36, 37, 64, 65, 9, 40, 66, 4, 41, 67, 42, 43, 68, 10, 76, 77, 38, 39, 78,
        5, 79, 56, 11, 57, 58, 59, 69, 20, 12, 32, 33, 70, 71, 34, 48, 35, 6, 49, 60, 13, 61, 24, 25,
        62, 21, 80, 63, 26, 50, 7, 14, 51, 27, 22, 52, 53, 23, 54, 15, 28, 55, 29, 30, 31, 16, 17, 18,
        19,
    ),
    (
        2, 1, 0, 8, 76, 77, 3, 78, 4, 79, 9, 40, 41, 56, 42, 57, 43, 58, 10, 59, 20, 60, 21, 68,
        5, 22, 69, 16, 11, 70, 28, 71, 23, 48, 17, 49, 18, 50, 12, 19, 32, 51, 33, 61, 29, 62, 6, 34,
        63, 30, 31, 13, 64, 65, 35, 66, 80, 67, 7, 14, 36, 37, 52, 53, 38, 54, 39, 55, 15, 24, 25, 26,
        27,
    ),
    (
        2, 0, 1, 8, 3, 40, 41, 4, 42, 43, 9, 76, 77, 28, 78, 29, 79, 30, 48, 10, 49, 24, 36, 50,
        31, 51, 5, 25, 52, 26, 11, 68, 27, 69, 37, 70, 20, 71, 38, 12, 64, 39, 65, 21, 66, 22, 6, 67,
        23, 53, 16, 54, 13, 55, 17, 18, 60, 80, 19, 61, 62, 7, 14, 32, 33, 63, 34, 35, 15, 56, 57, 58,
        59,
    ),
    (
        0, 1, 3, 8, 2, 64, 65, 36, 37, 4, 66, 38, 67, 9, 32, 39, 33, 34, 35, 10, 76, 77, 20, 78,
        28, 5, 79, 21, 22, 11, 68, 69, 23, 70, 29, 71, 30, 60, 31, 12, 61, 24, 62, 25, 63, 26, 6, 56,
        27, 57, 16, 58, 13, 59, 40, 41, 42, 80, 43, 7, 14, 17, 52, 18, 53, 54, 19, 55, 15, 48, 49, 50,
        51,
    ),
    (
        3, 2, 0, 8, 40, 41, 1, 42, 76, 77, 4, 43, 56, 9, 28, 57, 36, 58, 29, 59, 30, 78, 31, 10,
        79, 37, 38, 68, 5, 39, 69, 70, 32, 11, 71, 33, 34, 60, 35, 61, 24, 62, 12, 20, 63, 21, 22, 23,
        13, 64, 65, 25, 66, 16, 67, 26, 27, 14, 48, 49, 17, 18, 50, 19, 51, 15, 52, 53, 54, 55, 6, 80,
        7,
    ),
    (
        2, 0, 3, 8, 1, 36, 37, 64, 65, 4, 38, 66, 39, 9, 68, 40, 67, 41, 69, 42, 76, 43, 77, 10,
        24, 78, 25, 79, 5, 26, 70, 32, 71, 11, 28, 29, 30, 31, 12, 48, 49, 27, 33, 50, 34, 51, 35, 52,
        13, 53, 16, 17, 54, 18, 55, 19, 56, 14, 57, 58, 59, 60, 15, 61, 20, 21, 62, 22, 63, 23, 6, 80,
        7,
    ),
    (
        3, 1, 0, 8, 2, 76, 77, 36, 37, 4, 78, 38, 79, 9, 39, 56, 32, 57, 33, 58, 34, 64, 40, 10,
        59, 28, 65, 29, 5, 68, 30, 69, 31, 11, 70, 35, 71, 41, 66, 42, 67, 43, 12, 60, 24, 61, 25, 62,
        26, 63, 27, 13, 20, 21, 14, 22, 23, 48, 49, 15, 16, 50, 17, 18, 51, 19, 52, 6, 53, 54, 55, 80,
        7,
    ),
    (
        3, 0, 1, 8, 2, 76, 77, 40, 41, 4, 78, 42, 79, 9, 36, 64, 37, 65, 38, 66, 39, 67, 43, 10,
        48, 32, 49, 33, 5, 50, 34, 56, 35, 11, 51, 57, 68, 69, 12, 70, 24, 25, 71, 26, 58, 27, 59, 13,
        28, 29, 60, 61, 30, 62, 31, 63, 16, 14, 17, 52, 53, 18, 54, 19, 55, 15, 20, 21, 6, 22, 23, 80,
        7,
    ),
    (
        1, 3, 0, 8, 2, 36, 37, 64, 65, 4, 38, 66, 39, 9, 67, 32, 56, 33, 57, 34, 58, 35, 48, 10,
        49, 50, 5, 52, 28, 53, 11, 29, 76, 30, 77, 31, 78, 79, 12, 40, 41, 60, 42, 61, 43, 62, 63, 13,
        54, 55, 59, 24, 25, 14, 51, 26, 27, 68, 16, 17, 15, 69, 18, 70, 19, 71, 20, 6, 21, 22, 23, 80,
        7,
    ),
    (
        3, 1, 2, 8, 40, 41, 0, 42, 4, 43, 9, 76, 77, 78, 79, 20, 56, 21, 10, 36, 37, 48, 49, 38,
        50, 5, 39, 57, 22, 11, 23, 58, 59, 16, 17, 18, 12, 64, 65, 19, 66, 67, 68, 13, 32, 33, 69, 70,
        34, 71, 35, 52, 14, 24, 25, 53, 54, 26, 51, 27, 55, 15, 28, 29, 60, 30, 31, 61, 6, 62, 63, 80,
        7,
    ),
    (
        0, 2, 3, 8, 1, 76, 77, 4, 78, 79, 9, 28, 29, 30, 68, 31, 69, 10, 24, 40, 70, 25, 71, 5,
        26, 48, 27, 11, 64, 65, 41, 42, 66, 43, 67, 49, 16, 12, 50, 17, 51, 18, 20, 56, 57, 13, 32, 33,
        58, 34, 59, 35, 14, 36, 37, 38, 19, 39, 15, 60, 61, 21, 22, 62, 23, 63, 6, 52, 53, 54, 55, 80,
        7,
    ),
    (
        2, 3, 0, 8, 1, 36, 37, 76, 77, 4, 38, 78, 39, 9, 79, 32, 68, 33, 69, 34, 70, 35, 71, 10,
        20, 64, 21, 65, 5, 22, 66, 23, 67, 11, 24, 60, 25, 61, 26, 62, 28, 63, 12, 40, 41, 42, 43, 13,
        56, 57, 16, 17, 58, 27, 59, 18, 14, 48, 49, 29, 30, 50, 31, 51, 19, 15, 52, 6, 53, 54, 55, 80,
        7,
    ),
    (
        8, 0, 40, 41, 1, 42, 2, 3, 43, 9, 76, 77, 36, 4, 28, 78, 37, 79, 29, 10, 30, 64, 65, 31,
        66, 38, 5, 67, 39, 60, 11, 61, 32, 33, 68, 34, 62, 16, 63, 17, 12, 69, 18, 70, 19, 71, 35, 6,
        52, 24, 53, 25, 54, 13, 20, 56, 26, 57, 80, 21, 58, 22, 7, 14, 59, 48, 23, 27, 49, 50, 15, 51,
        55,
    ),
    (
        3, 1, 76, 8, 77, 78, 0, 2, 79, 36, 37, 64, 4, 38, 9, 39, 65, 66, 40, 67, 41, 68, 42, 69,
        10, 70, 43, 32, 71, 24, 5, 56, 25, 57, 11, 26, 58, 27, 59, 33, 52, 34, 53, 35, 12, 60, 20, 54,
        28, 55, 29, 6, 61, 30, 62, 31, 63, 13, 21, 22, 80, 23, 48, 7, 14, 49, 50, 51, 15, 16, 17, 18,
        19,
    ),
    (
        2, 0, 3, 8, 1, 64, 65, 40, 41, 4, 66, 42, 67, 9, 43, 68, 36, 69, 32, 70, 33, 71, 34, 10,
        76, 35, 77, 37, 5, 78, 38, 79, 39, 11, 56, 28, 57, 16, 58, 17, 59, 18, 12, 60, 19, 61, 29, 62,
        30, 6, 52, 31, 63, 13, 53, 20, 21, 54, 22, 80, 55, 23, 7, 14, 24, 25, 26, 27, 15, 48, 49, 50,
        51,
    ),
    (
        3, 1, 0, 8, 2, 64, 65, 40, 41, 4, 66, 42, 67, 9, 43, 56, 36, 57, 37, 58, 38, 60, 39, 10,
        61, 24, 62, 25, 5, 63, 26, 68, 11, 69, 27, 28, 70, 29, 71, 20, 48, 30, 12, 49, 21, 50, 22, 51,
        23, 6, 52, 31, 53, 32, 54, 33, 13, 59, 34, 55, 35, 80, 76, 7, 14, 16, 77, 78, 17, 79, 18, 19,
        15,
    ),
)
ARRIVAL = (
    (
        11, 8, 9, 15, 10, 12, 13, 14,
    ),
    (
        11, 10, 9, 15, 12, 8, 13, 14,
    ),
    (
        12, 13, 15, 11, 10, 9, 14, 8,
    ),
    (
        12, 11, 15, 13, 10, 14, 9, 8,
    ),
    (
        12, 15, 13, 8, 9, 14, 10, 11,
    ),
    (
        10, 8, 13, 11, 12, 14, 15, 9,
    ),
    (
        13, 12, 9, 14, 8, 11, 15, 10,
    ),
    (
        8, 9, 13, 12, 10, 11, 15, 14,
    ),
    (
        11, 10, 13, 9, 8, 12, 14, 15,
    ),
    (
        10, 11, 13, 9, 8, 12, 14, 15,
    ),
    (
        13, 11, 12, 10, 8, 14, 15, 9,
    ),
    (
        15, 13, 12, 11, 14, 10, 8, 9,
    ),
    (
        13, 10, 14, 15, 11, 12, 8, 9,
    ),
    (
        14, 8, 15, 13, 9, 12, 11, 10,
    ),
    (
        9, 8, 10, 15, 13, 11, 12, 14,
    ),
    (
        9, 13, 10, 11, 8, 15, 12, 14,
    ),
)


def pick(values, row):
    value = jnp.int32(values[0])
    for c in range(1, len(values)):
        value = jnp.where(row == c, jnp.int32(values[c]), value)
    return value


def packed(codes, bits):
    return sum(code << (bits * i) for i, code in enumerate(codes))


def kernel(
    tokens, gain, weight, local, base, momentum,
    out, out_base, out_mom,
    tok, xg, gvec, wl, wr, prod, sbuf, rbuf, sq, sqr, rsf,
    bv, lv, mv, vbuf, frecv, fsum, xr, fown, fall,
    near_sem, far_sem, group_sem, load_sem, xs, xrs, zs, zr, qs, qr, fs, fr, hs, hr, gs, gr,
):
    rep = lax.axis_index("replica")
    t = lax.axis_index("tensor")
    f = lax.axis_index("fsdp")
    place = lax.rem(t + 4 * f, RING)
    row = f * RING + place
    other = (1 - f) * RING + lax.rem(place + 4, RING)
    y = rep // 4
    xh = lax.rem(rep // 2, 2)
    core = lax.rem(rep, 2)
    k = y * 2 + core

    def member(delta):
        p = lax.rem(k + delta, RING)
        return p, ((p // 2) * 4 + xh * 2 + lax.rem(p, 2), t, f)

    def on_ring(delta):
        return (rep, lax.rem(t + delta, RING), f)

    x_dev = (rep, t, 1 - f)
    h_dev = (y * 4 + (1 - xh) * 2 + core, t, f)

    def told(sem, count):
        @pl.when(count > 0)
        def _():
            pl.semaphore_wait(sem, count)

    barrier = pltpu.get_barrier_semaphore()
    pl.semaphore_signal(barrier, inc=1, device_id=x_dev, device_id_type=MESH)

    parts = [pick([codes[j] - 8 for codes in ARRIVAL], other) for j in range(8)]
    part_loads = [
        pltpu.make_async_copy(
            weight.at[0, :, pl.ds(pl.multiple_of(parts[j] * 128, 128), 128)], wl.at[parts[j]], load_sem.at[5 + j]
        )
        for j in range(8)
    ]
    for j in range(FIRST):
        part_loads[j].start()

    def on_pair(mine, theirs, sem, dev):
        @pl.when(mine < theirs if sem is barrier else mine > theirs)
        def _():
            pl.semaphore_signal(sem, inc=1, device_id=dev, device_id_type=MESH)

    def tell(near, far, group):
        for delta in range(1, RING):
            sem = near if delta in (1, RING - 1) else far
            on_pair(t, lax.rem(t + delta, RING), sem, on_ring(delta))
        for delta in range(1, RING):
            p, dev = member(delta)
            on_pair(k, p, group, dev)
        on_pair(xh, 1 - xh, group, h_dev)

    tell(barrier, barrier, barrier)
    loads = [
        pltpu.make_async_copy(src, dst, load_sem.at[i])
        for i, (src, dst) in enumerate(
            ((tokens, tok), (gain, gvec), (base, bv), (local.at[0], lv), (momentum, mv))
        )
    ]
    pl.semaphore_wait(barrier, 1 + t + k + xh)

    x_copies = []
    for j in range(8):
        x_copies.append(
            pltpu.make_async_remote_copy(
                src_ref=wl.at[parts[j]],
                dst_ref=wr.at[j],
                send_sem=xs.at[j],
                recv_sem=xrs.at[j],
                device_id=x_dev,
                device_id_type=MESH,
            )
        )
    for j in range(FIRST):
        part_loads[j].wait()
        x_copies[j].start()
    for load in loads + part_loads[FIRST:]:
        load.start()

    tell(near_sem, far_sem, group_sem)

    def sq_copy(delta):
        return pltpu.make_async_remote_copy(
            src_ref=sq, dst_ref=sqr.at[delta - 1], send_sem=qs.at[delta - 1], recv_sem=qr.at[delta - 1],
            device_id=on_ring(delta), device_id_type=MESH,
        )

    def rs_copy(delta):
        p, dev = member(delta)
        return pltpu.make_async_remote_copy(
            src_ref=vbuf.at[p], dst_ref=frecv.at[delta - 1], send_sem=fs.at[delta - 1],
            recv_sem=fr.at[delta - 1], device_id=dev, device_id_type=MESH,
        )

    def h_copy():
        return pltpu.make_async_remote_copy(
            src_ref=fsum, dst_ref=xr, send_sem=hs.at[0], recv_sem=hr.at[0], device_id=h_dev, device_id_type=MESH
        )

    core_dev = (y * 4 + xh * 2 + 1 - core, t, f)
    step_core = 1 - 2 * core

    def ag_copy(delta):
        return pltpu.make_async_remote_copy(
            src_ref=fown, dst_ref=fall.at[delta - 1], send_sem=gs.at[delta - 1], recv_sem=gr.at[delta - 1],
            device_id=member(delta)[1], device_id_type=MESH,
        )

    def core_copy(delta):
        slot = lax.rem(delta + step_core + RING, RING) - 1
        return pltpu.make_async_remote_copy(
            src_ref=fall.at[delta - 1] if delta else fown, dst_ref=fall.at[slot], send_sem=gs.at[delta],
            recv_sem=gr.at[slot], device_id=core_dev, device_id_type=MESH,
        )

    def z_copy(idx, h, dev):
        return pltpu.make_async_remote_copy(
            src_ref=sbuf.at[idx, h], dst_ref=rbuf.at[idx, h], send_sem=zs.at[idx * CUT + h],
            recv_sem=zr.at[idx * CUT + h], device_id=dev, device_id_type=MESH,
        )

    loads[2].wait()
    loads[3].wait()

    @pl.loop(0, RING)
    def _(p):
        for g in range(FCOLS // G):
            cols = pl.ds(pl.multiple_of(p * FCOLS + g * G, G), G)
            grad = bv[:, cols] - lv[:, cols]
            top = jnp.max(jnp.abs(grad), axis=1, keepdims=True)
            scale = (top + SCALE_EPS).astype(BF16).astype(F32)
            level = (grad / scale).astype(BF16).astype(F32)
            vbuf[p, :, g * G : (g + 1) * G] = (level * scale).astype(BF16)

    words = [
        pick([packed(codes[n : n + 4], 7) for codes in ORDER], row) for n in range(0, len(ORDER[0]), 4)
    ]
    arrival = pick([packed([u - 8 for u in parts], 3) for parts in ARRIVAL], row)

    loads[0].wait()
    loads[1].wait()

    @pl.loop(0, TOK // 128)
    def _(i):
        rows = pl.ds(pl.multiple_of(i * 128, 128), 128)
        xg[rows, :] = (tok[rows, :].astype(F32) * gvec[...]).astype(BF16)

    for j in range(FIRST, 8):
        part_loads[j].wait()

    @pl.when(t >= RING // 2)
    def _():
        for copy in x_copies[FIRST:]:
            copy.start()

    told(group_sem, RING - 1 - k + 1 - xh)
    for delta in range(1, RING):
        rs_copy(delta).start()

    near = jnp.where(t == 0, 2, jnp.where(t == RING - 1, 0, 1))
    told(near_sem, near)

    def own_product(q):
        both = jnp.concatenate([wl[2 * q], wl[2 * q + 1]], axis=1)
        res = jnp.dot(xg[...], both, preferred_element_type=F32)
        prod[2 * q] = res[:, :128].reshape(CUT, PART, 128)
        prod[2 * q + 1] = res[:, 128:].reshape(CUT, PART, 128)

    def other_product(j):
        pltpu.make_async_remote_copy(
            src_ref=wr.at[j], dst_ref=wr.at[j], send_sem=xs.at[j], recv_sem=xrs.at[j],
            device_id=x_dev, device_id_type=MESH,
        ).wait_recv()
        u = 8 + lax.bitwise_and(lax.shift_right_logical(arrival, 3 * j), jnp.int32(7))

        prod[u] = jnp.dot(xg[...], wr[j], preferred_element_type=F32).reshape(CUT, PART, 128)

    def pass_on(code):
        h = lax.rem(code, CUT)
        idx = code // CUT
        up = idx // 8
        r = lax.rem(idx, 8) // 2 + 1
        s = lax.rem(idx, 2)
        step = 2 * up - 1
        u = 2 * lax.rem(place + step * r + RING, RING) + s
        dev = on_ring(step + RING)
        first = (r == 4) | ((r == 3) & (s == 1 - up))

        @pl.when(first)
        def _():
            @pl.loop(0, PART // 128)
            def _(i):
                rows = pl.ds(pl.multiple_of(i * 128, 128), 128)
                sbuf[idx, h, rows, :] = prod[u, h, rows, :].astype(BF16)

        @pl.when(jnp.logical_not(first))
        def _():
            z_copy(idx + 2, h, dev).wait_recv()

            @pl.loop(0, PART // 128)
            def _(i):
                rows = pl.ds(pl.multiple_of(i * 128, 128), 128)
                sbuf[idx, h, rows, :] = (
                    prod[u, h, rows, :] + rbuf[idx + 2, h, rows, :].astype(F32)
                ).astype(BF16)

        z_copy(idx, h, dev).start()

    def squares():
        ones = jnp.ones((16, FEAT), BF16)
        sub = lax.broadcasted_iota(jnp.int32, (8, 128), 0)
        acc = jnp.zeros((8, 128), F32)
        for i in range(TOK // 256):
            x = tok[i * 256 : (i + 1) * 256, :].astype(F32)
            x2 = x * x
            hi = x2.astype(BF16)
            lo = (x2 - hi.astype(F32)).astype(BF16)
            dims = (((1,), (1,)), ((), ()))
            row = lax.dot_general(ones, hi, dims, preferred_element_type=F32)
            row = row + lax.dot_general(ones, lo, dims, preferred_element_type=F32)
            for g in range(2):
                acc = acc + jnp.where(sub == 2 * i + g, row[0:8, g * 128 : (g + 1) * 128], 0.0)
        sq[...] = acc
        told(far_sem, RING - 1 - t - near)
        for delta in range(1, RING):
            sq_copy(delta).start()

    def fragment_sum():
        for delta in range(1, RING):
            rs_copy(delta).wait_recv()
        total = vbuf[k].astype(F32)
        for delta in range(1, RING):
            total = total + frecv[delta - 1].astype(F32)
        fsum[...] = total.astype(BF16)
        h_copy().start()

        @pl.when(t < RING // 2)
        def _():
            for copy in x_copies[FIRST:]:
                copy.start()

    def fragment_spread():
        h_copy().wait_recv()
        fown[...] = (fsum[...].astype(F32) + xr[...].astype(F32)).astype(BF16)
        for delta in (2, 4, 6):
            ag_copy(delta).start()
        core_copy(0).start()

    def fragment_pass():
        for delta in (2, 4, 6):
            ag_copy(delta).wait_recv()
            core_copy(delta).start()

    def fragment_end():
        for delta in (1, 3, 5, 7):
            ag_copy(delta).wait_recv()
        loads[4].wait()

        for delta in range(RING):
            p = lax.rem(k + RING - delta, RING)
            cols = pl.ds(pl.multiple_of(p * FCOLS, FCOLS), FCOLS)
            piece = fown[...] if delta == 0 else fall[delta - 1]
            average = piece.astype(F32) / REPLICAS
            new_mom = OUTER_MOMENTUM * mv[:, cols] + average
            out_mom[:, cols] = new_mom
            out_base[:, cols] = bv[:, cols] - OUTER_RATE * (average + OUTER_MOMENTUM * new_mom)

        total = sq[...]
        for delta in range(1, RING):
            sq_copy(delta).wait_recv()
            total = total + sqr[delta - 1]
        rs = lax.rsqrt(total / WIDTH + NORM_EPS)
        for g in range(TOK // 128):
            rsf[g * 128 // PART, g * 128 % PART : g * 128 % PART + 128, :] = jnp.broadcast_to(rs[g : g + 1, :], (128, 128)).T

    @pl.loop(0, len(ORDER[0]))
    def _(n):
        word = words[0]
        for i in range(1, len(words)):
            word = jnp.where(n // 4 == i, words[i], word)
        code = lax.bitwise_and(lax.shift_right_logical(word, 7 * lax.rem(n, 4)), jnp.int32(127))

        @pl.when(code < 4)
        def _():
            own_product(code)

        @pl.when((code >= 8) & (code < 16))
        def _():
            other_product(code - 8)

        @pl.when((code >= 16) & (code < 16 + 16 * CUT))
        def _():
            pass_on(code - 16)

        @pl.when(code == 4)
        def _():
            squares()

        @pl.when(code == 5)
        def _():
            fragment_sum()

        @pl.when(code == 6)
        def _():
            fragment_spread()

        @pl.when(code == 7)
        def _():
            fragment_end()

        @pl.when(code == 16 + 16 * CUT)
        def _():
            fragment_pass()

    for h in range(CUT):
        for s in range(2):
            z_copy(s, h, on_ring(1)).wait_recv()
            z_copy(8 + s, h, on_ring(1)).wait_recv()

            @pl.loop(0, PART // 128)
            def _(i):
                rows = pl.ds(pl.multiple_of(i * 128, 128), 128)
                total = prod[2 * place + s, h, rows, :] + rbuf[s, h, rows, :].astype(F32)
                total = total + rbuf[8 + s, h, rows, :].astype(F32)
                out[pl.ds(pl.multiple_of(h * PART + i * 128, 128), 128), s * 128 : (s + 1) * 128] = (total * rsf[h, rows, :]).astype(BF16)

    for copy in x_copies:
        copy.wait_send()
    for idx in range(16):
        if idx in (6 + 1, 8 + 6):
            continue
        for h in range(CUT):
            z_copy(idx, h, on_ring(1)).wait_send()
    for delta in range(1, RING):
        sq_copy(delta).wait_send()
        rs_copy(delta).wait_send()
    for delta in (2, 4, 6):
        ag_copy(delta).wait_send()
        core_copy(delta).wait_send()
    core_copy(0).wait_send()
    h_copy().wait_send()


def write_out(a, b, c, a_out, b_out, c_out, sem):
    copies = []
    for src, dst in ((a, a_out), (b, b_out), (c, c_out)):
        rows = src.shape[0] // 2
        for i in range(2):
            part = pl.ds(i * rows, rows)
            copies.append(pltpu.make_async_copy(src.at[part], dst.at[part], sem.at[len(copies)]))
            copies[-1].start()
    for copy in copies:
        copy.wait()


def body(tokens, gain, weight, local, base, momentum):
    dma = pltpu.SemaphoreType.DMA
    any_spec = pl.BlockSpec(memory_space=pltpu.HBM)
    parts = pl.pallas_call(
        kernel,
        out_shape=(
            pltpu.VMEM((TOK, 256), BF16),
            pltpu.VMEM(base.shape, F32),
            pltpu.VMEM(base.shape, F32),
        ),
        in_specs=[any_spec] * 6,
        out_specs=[pl.BlockSpec(memory_space=pltpu.VMEM)] * 3,
        scratch_shapes=[
            pltpu.VMEM((TOK, FEAT), BF16),
            pltpu.VMEM((TOK, FEAT), BF16),
            pltpu.VMEM((1, FEAT), F32),
            pltpu.VMEM((8, FEAT, 128), BF16),
            pltpu.VMEM((8, FEAT, 128), BF16),
            pltpu.VMEM((16, CUT, PART, 128), F32),
            pltpu.VMEM((16, CUT, PART, 128), BF16),
            pltpu.VMEM((16, CUT, PART, 128), BF16),
            pltpu.VMEM((8, 128), F32),
            pltpu.VMEM((RING - 1, 8, 128), F32),
            pltpu.VMEM((CUT, PART, 128), F32),
            pltpu.VMEM((FROWS, WIDTH), F32),
            pltpu.VMEM((FROWS, WIDTH), F32),
            pltpu.VMEM((FROWS, WIDTH), F32),
            pltpu.VMEM((RING, FROWS, FCOLS), BF16),
            pltpu.VMEM((RING - 1, FROWS, FCOLS), BF16),
            pltpu.VMEM((FROWS, FCOLS), BF16),
            pltpu.VMEM((FROWS, FCOLS), BF16),
            pltpu.VMEM((FROWS, FCOLS), BF16),
            pltpu.VMEM((RING - 1, FROWS, FCOLS), BF16),
            pltpu.SemaphoreType.REGULAR,
            pltpu.SemaphoreType.REGULAR,
            pltpu.SemaphoreType.REGULAR,
            dma((5 + 8,)),
            dma((8,)),
            dma((8,)),
            dma((16 * CUT,)),
            dma((16 * CUT,)),
            dma((RING - 1,)),
            dma((RING - 1,)),
            dma((RING - 1,)),
            dma((RING - 1,)),
            dma((1,)),
            dma((1,)),
            dma((RING - 1,)),
            dma((RING - 1,)),
        ],
        compiler_params=pltpu.CompilerParams(
            collective_id=0, has_side_effects=True, vmem_limit_bytes=50 * 1024 * 1024
        ),
    )(tokens, gain.reshape(1, FEAT), weight, local, base, momentum)
    return pl.pallas_call(
        write_out,
        out_shape=tuple(jax.ShapeDtypeStruct(part.shape, part.dtype) for part in parts),
        in_specs=[pl.BlockSpec(memory_space=pl.ANY)] * 3,
        out_specs=[any_spec] * 3,
        scratch_shapes=[dma((6,))],
        compiler_params=pltpu.CompilerParams(vmem_limit_bytes=1024 * 1024),
    )(*parts)


def solution(mesh):
    placed = (
        P(("replica", "fsdp"), "tensor"),
        P("tensor"),
        P("replica", "tensor", "fsdp"),
        P("replica", ("tensor", "fsdp"), None),
        P(("tensor", "fsdp"), None),
        P(("tensor", "fsdp"), None),
    )
    return jax.shard_map(
        body,
        mesh=mesh,
        in_specs=placed,
        out_specs=(
            P(("replica", "fsdp"), "tensor"),
            P(("tensor", "fsdp"), None),
            P(("tensor", "fsdp"), None),
        ),
        check_vma=False,
    )
```

```python
import jax
import jax.numpy as jnp
from jax import lax
from jax.experimental import pallas as pl
from jax.experimental.pallas import tpu as pltpu
from jax.sharding import PartitionSpec as P

F32 = jnp.float32
BF16 = jnp.bfloat16
MESH = pl.DeviceIdType.MESH

G = 128
OUTER_MOMENTUM = 0.9
OUTER_RATE = 0.7
NORM_EPS = 1e-05
SCALE_EPS = 1e-06
REPLICAS = 16
WIDTH = 8192
RING = 8
FIRST = 5
TOK = 1024
FEAT = 1024
COLS = 48
CUT = 4
PART = TOK // CUT
FROWS = 48
FCOLS = 1024

ORDER = (
    (
        0, 8, 1, 3, 64, 65, 2, 66, 4, 9, 67, 76, 40, 41, 77, 42, 78, 43, 68, 10, 85, 69, 32, 33,
        70, 34, 79, 5, 35, 60, 11, 36, 61, 37, 62, 38, 71, 39, 63, 12, 24, 56, 25, 57, 26, 58, 27, 6,
        48, 59, 52, 13, 49, 53, 80, 50, 7, 14, 51, 54, 28, 29, 55, 30, 31, 81, 82, 83, 84, 20, 21, 22,
        23, 16, 17, 18, 19,
    ),
    (
        2, 3, 1, 8, 0, 76, 77, 4, 78, 56, 9, 40, 57, 41, 42, 58, 43, 59, 79, 10, 32, 33, 85, 34,
        60, 35, 5, 20, 61, 11, 21, 62, 68, 22, 69, 23, 70, 71, 12, 16, 64, 63, 17, 65, 6, 18, 66, 19,
        67, 48, 13, 36, 49, 37, 38, 50, 80, 39, 51, 52, 7, 14, 28, 29, 53, 54, 30, 55, 31, 81, 82, 83,
        84, 24, 25, 26, 27,
    ),
    (
        2, 1, 0, 8, 3, 40, 41, 4, 42, 43, 9, 68, 69, 28, 70, 29, 48, 30, 49, 31, 10, 64, 20, 85,
        65, 21, 66, 22, 5, 67, 23, 11, 50, 24, 51, 36, 71, 25, 52, 26, 12, 76, 27, 77, 37, 78, 38, 6,
        79, 16, 53, 39, 54, 17, 13, 32, 55, 33, 80, 34, 35, 7, 14, 60, 61, 18, 19, 62, 63, 81, 82, 83,
        84, 56, 57, 58, 59,
    ),
    (
        3, 1, 0, 8, 2, 36, 37, 4, 38, 76, 77, 39, 9, 78, 28, 79, 29, 30, 31, 10, 32, 64, 65, 85,
        33, 66, 34, 67, 5, 35, 56, 11, 57, 40, 41, 58, 42, 59, 24, 12, 43, 25, 16, 68, 6, 17, 69, 18,
        70, 19, 13, 71, 60, 26, 61, 27, 80, 62, 20, 63, 21, 7, 14, 22, 23, 52, 53, 81, 82, 83, 84, 54,
        55, 48, 49, 50, 51,
    ),
    (
        0, 3, 1, 8, 36, 37, 2, 38, 76, 77, 4, 39, 78, 9, 68, 40, 41, 79, 42, 69, 43, 70, 28, 10,
        71, 85, 32, 33, 34, 5, 29, 11, 56, 57, 35, 58, 24, 59, 25, 26, 12, 48, 27, 49, 50, 30, 51, 31,
        20, 13, 16, 64, 65, 17, 66, 18, 67, 19, 60, 14, 21, 61, 22, 62, 23, 63, 81, 82, 83, 84, 52, 53,
        54, 55, 6, 80, 7,
    ),
    (
        0, 3, 1, 8, 76, 77, 2, 78, 36, 37, 4, 79, 38, 9, 68, 39, 64, 40, 69, 41, 70, 42, 65, 10,
        28, 85, 71, 43, 66, 32, 67, 33, 5, 34, 11, 60, 61, 35, 62, 29, 63, 30, 48, 31, 12, 49, 24, 50,
        25, 51, 26, 27, 13, 56, 14, 16, 17, 57, 58, 18, 59, 19, 52, 20, 53, 81, 82, 83, 84, 54, 21, 22,
        55, 23, 6, 80, 7,
    ),
    (
        2, 1, 3, 8, 76, 77, 0, 78, 40, 41, 4, 79, 42, 9, 43, 68, 69, 36, 70, 32, 71, 33, 60, 10,
        34, 85, 64, 35, 61, 37, 62, 38, 5, 65, 39, 11, 63, 66, 67, 16, 52, 17, 12, 53, 18, 54, 19, 55,
        20, 56, 13, 24, 25, 57, 26, 58, 27, 59, 28, 14, 29, 30, 31, 21, 81, 82, 83, 84, 48, 49, 22, 50,
        51, 6, 23, 80, 7,
    ),
    (
        0, 1, 3, 8, 2, 76, 77, 4, 78, 40, 41, 68, 9, 42, 69, 43, 70, 71, 79, 10, 32, 33, 64, 85,
        34, 65, 35, 66, 5, 24, 67, 11, 56, 25, 26, 60, 27, 61, 28, 57, 12, 16, 62, 17, 58, 18, 59, 19,
        63, 13, 36, 52, 37, 53, 38, 54, 39, 48, 14, 49, 29, 30, 50, 20, 51, 21, 55, 81, 82, 83, 84, 22,
        23, 31, 6, 80, 7,
    ),
    (
        0, 1, 3, 8, 40, 41, 2, 42, 64, 65, 4, 43, 66, 9, 67, 56, 57, 58, 10, 68, 32, 33, 69, 85,
        34, 70, 35, 48, 5, 49, 11, 36, 37, 50, 38, 51, 39, 71, 59, 12, 28, 29, 60, 30, 31, 24, 13, 76,
        77, 25, 78, 26, 79, 27, 61, 14, 62, 63, 16, 17, 81, 82, 18, 83, 84, 52, 19, 53, 20, 6, 21, 54,
        22, 55, 23, 80, 7,
    ),
    (
        2, 1, 0, 8, 3, 76, 77, 4, 78, 79, 9, 40, 41, 56, 42, 57, 43, 58, 16, 59, 10, 48, 20, 85,
        17, 49, 21, 50, 5, 18, 60, 11, 36, 61, 37, 62, 38, 39, 12, 32, 64, 65, 33, 66, 34, 63, 35, 51,
        13, 52, 22, 23, 67, 19, 24, 14, 25, 68, 69, 26, 70, 27, 71, 53, 81, 28, 82, 29, 83, 30, 84, 54,
        55, 31, 6, 80, 7,
    ),
    (
        2, 1, 0, 8, 76, 77, 3, 78, 4, 79, 9, 24, 64, 65, 28, 66, 25, 67, 29, 10, 48, 26, 68, 85,
        27, 49, 50, 5, 51, 11, 40, 41, 69, 42, 70, 43, 71, 30, 52, 12, 31, 53, 54, 56, 13, 32, 33, 57,
        58, 34, 55, 35, 14, 36, 37, 59, 38, 39, 20, 81, 60, 82, 61, 83, 62, 84, 21, 22, 63, 23, 6, 16,
        17, 18, 19, 80, 7,
    ),
    (
        0, 3, 1, 8, 2, 32, 76, 77, 36, 4, 33, 78, 37, 79, 9, 34, 35, 20, 56, 21, 10, 64, 65, 22,
        85, 66, 23, 67, 38, 5, 57, 39, 11, 68, 69, 70, 16, 71, 12, 40, 41, 58, 59, 42, 43, 17, 13, 18,
        60, 61, 19, 62, 28, 63, 29, 14, 48, 49, 30, 31, 50, 24, 51, 25, 81, 82, 83, 84, 26, 27, 52, 6,
        53, 54, 55, 80, 7,
    ),
    (
        1, 8, 0, 2, 3, 40, 41, 4, 9, 42, 43, 76, 77, 28, 78, 29, 79, 30, 68, 10, 31, 85, 64, 20,
        65, 21, 66, 5, 22, 67, 11, 23, 69, 16, 70, 24, 71, 17, 12, 56, 57, 18, 19, 58, 25, 59, 6, 26,
        60, 27, 61, 36, 13, 62, 37, 63, 38, 48, 80, 39, 49, 7, 14, 50, 51, 32, 33, 52, 34, 53, 35, 54,
        81, 82, 83, 84, 55,
    ),
    (
        2, 0, 3, 8, 1, 64, 65, 36, 37, 4, 66, 38, 67, 9, 39, 76, 28, 77, 29, 68, 30, 69, 31, 10,
        70, 85, 24, 71, 32, 78, 25, 5, 79, 26, 11, 56, 27, 57, 33, 58, 34, 59, 35, 12, 60, 20, 61, 16,
        62, 17, 6, 63, 18, 48, 19, 49, 40, 13, 52, 41, 53, 42, 80, 54, 43, 55, 7, 14, 50, 21, 22, 51,
        81, 82, 83, 84, 23,
    ),
    (
        1, 2, 3, 8, 36, 37, 0, 38, 76, 77, 4, 39, 78, 9, 79, 32, 40, 64, 33, 65, 34, 66, 35, 10,
        85, 41, 67, 60, 42, 56, 43, 5, 61, 28, 11, 62, 24, 63, 25, 57, 26, 58, 27, 48, 12, 16, 49, 17,
        50, 18, 51, 6, 19, 52, 29, 53, 30, 13, 54, 20, 55, 21, 59, 80, 22, 68, 7, 14, 23, 31, 69, 70,
        71, 81, 82, 83, 84,
    ),
    (
        3, 2, 0, 8, 40, 41, 1, 42, 64, 65, 4, 43, 66, 9, 36, 67, 37, 76, 38, 77, 39, 78, 32, 10,
        56, 85, 57, 33, 34, 58, 35, 59, 5, 79, 11, 24, 52, 25, 68, 26, 53, 27, 54, 12, 28, 55, 29, 69,
        30, 70, 31, 6, 71, 20, 48, 21, 13, 22, 49, 50, 23, 80, 16, 17, 7, 14, 18, 19, 51, 60, 61, 81,
        82, 83, 84, 62, 63,
    ),
)
ARRIVAL = (
    (
        9, 8, 10, 11, 12, 13, 15, 14,
    ),
    (
        11, 10, 12, 9, 8, 13, 15, 14,
    ),
    (
        12, 11, 10, 15, 13, 14, 9, 8,
    ),
    (
        15, 10, 12, 14, 13, 11, 9, 8,
    ),
    (
        13, 15, 9, 12, 10, 14, 8, 11,
    ),
    (
        13, 12, 14, 15, 11, 9, 8, 10,
    ),
    (
        10, 15, 9, 13, 11, 8, 12, 14,
    ),
    (
        10, 12, 8, 11, 13, 9, 15, 14,
    ),
    (
        8, 12, 10, 11, 13, 9, 14, 15,
    ),
    (
        11, 10, 12, 13, 8, 14, 9, 15,
    ),
    (
        13, 10, 11, 12, 8, 14, 15, 9,
    ),
    (
        15, 10, 12, 13, 14, 11, 8, 9,
    ),
    (
        15, 13, 14, 9, 12, 10, 11, 8,
    ),
    (
        9, 12, 8, 14, 15, 13, 11, 10,
    ),
    (
        15, 8, 9, 14, 10, 11, 13, 12,
    ),
    (
        9, 8, 10, 11, 13, 12, 15, 14,
    ),
)


def pick(values, row):
    value = jnp.int32(values[0])
    for c in range(1, len(values)):
        value = jnp.where(row == c, jnp.int32(values[c]), value)
    return value


def low(value, size):
    return lax.bitwise_and(value, jnp.int32(size - 1))


def packed(codes, bits):
    return sum(code << (bits * i) for i, code in enumerate(codes))


def kernel(
    tokens, gain, weight, local, base, momentum,
    out, out_base, out_mom,
    tok, xg, gvec, wl, wr, prod, sbuf, rbuf, sq, sqr, rsf,
    bv, lv, mv, vbuf, frecv, fsum, xr, fown, fall,
    near_sem, far_sem, group_sem, load_sem, xs, xrs, zs, zr, qs, qr, fs, fr, hs, hr, gs, gr,
):
    rep = lax.axis_index("replica")
    t = lax.axis_index("tensor")
    f = lax.axis_index("fsdp")
    place = lax.rem(t + 4 * f, RING)
    row = f * RING + place
    other = (1 - f) * RING + lax.rem(place + 4, RING)
    y = rep // 4
    xh = lax.rem(rep // 2, 2)
    core = lax.rem(rep, 2)
    k = y * 2 + core

    def member(delta):
        p = lax.rem(k + delta, RING)
        return p, ((p // 2) * 4 + xh * 2 + lax.rem(p, 2), t, f)

    def on_ring(delta):
        return (rep, lax.rem(t + delta, RING), f)

    x_dev = (rep, t, 1 - f)
    h_dev = (y * 4 + (1 - xh) * 2 + core, t, f)

    def told(sem, count):
        @pl.when(count > 0)
        def _():
            pl.semaphore_wait(sem, count)

    barrier = pltpu.get_barrier_semaphore()
    pl.semaphore_signal(barrier, inc=1, device_id=x_dev, device_id_type=MESH)

    parts = [pick([codes[j] - 8 for codes in ARRIVAL], other) for j in range(8)]
    part_loads = [
        pltpu.make_async_copy(
            weight.at[0, :, pl.ds(pl.multiple_of(parts[j] * 128, 128), 128)], wl.at[parts[j]], load_sem.at[5 + j]
        )
        for j in range(8)
    ]
    for j in range(FIRST):
        part_loads[j].start()

    def on_pair(mine, theirs, sem, dev):
        @pl.when(mine < theirs if sem is barrier else mine > theirs)
        def _():
            pl.semaphore_signal(sem, inc=1, device_id=dev, device_id_type=MESH)

    def tell(near, far, group):
        for delta in range(1, RING):
            sem = near if delta in (1, RING - 1) else far
            on_pair(t, lax.rem(t + delta, RING), sem, on_ring(delta))
        for delta in range(1, RING):
            p, dev = member(delta)
            on_pair(k, p, group, dev)
        on_pair(xh, 1 - xh, group, h_dev)

    tell(barrier, barrier, barrier)
    loads = [
        pltpu.make_async_copy(src, dst, load_sem.at[i])
        for i, (src, dst) in enumerate(
            ((tokens, tok), (gain, gvec), (base, bv), (local.at[0], lv), (momentum, mv))
        )
    ]
    pl.semaphore_wait(barrier, 1 + t + k + xh)

    x_copies = []
    for j in range(8):
        x_copies.append(
            pltpu.make_async_remote_copy(
                src_ref=wl.at[parts[j]],
                dst_ref=wr.at[j],
                send_sem=xs.at[j],
                recv_sem=xrs.at[j],
                device_id=x_dev,
                device_id_type=MESH,
            )
        )
    for j in range(FIRST):
        part_loads[j].wait()
        x_copies[j].start()
    for load in loads + part_loads[FIRST:]:
        load.start()

    tell(near_sem, far_sem, group_sem)

    def sq_copy(delta):
        return pltpu.make_async_remote_copy(
            src_ref=sq, dst_ref=sqr.at[delta - 1], send_sem=qs.at[delta - 1], recv_sem=qr.at[delta - 1],
            device_id=on_ring(delta), device_id_type=MESH,
        )

    def rs_copy(delta):
        p, dev = member(delta)
        return pltpu.make_async_remote_copy(
            src_ref=vbuf.at[p], dst_ref=frecv.at[delta - 1], send_sem=fs.at[delta - 1],
            recv_sem=fr.at[delta - 1], device_id=dev, device_id_type=MESH,
        )

    def h_copy():
        return pltpu.make_async_remote_copy(
            src_ref=fsum, dst_ref=xr, send_sem=hs.at[0], recv_sem=hr.at[0], device_id=h_dev, device_id_type=MESH
        )

    core_dev = (y * 4 + xh * 2 + 1 - core, t, f)
    step_core = 1 - 2 * core

    def ag_copy(delta):
        return pltpu.make_async_remote_copy(
            src_ref=fown, dst_ref=fall.at[delta - 1], send_sem=gs.at[delta - 1], recv_sem=gr.at[delta - 1],
            device_id=member(delta)[1], device_id_type=MESH,
        )

    def core_copy(delta):
        slot = lax.rem(delta + step_core + RING, RING) - 1
        return pltpu.make_async_remote_copy(
            src_ref=fall.at[delta - 1] if delta else fown, dst_ref=fall.at[slot], send_sem=gs.at[delta],
            recv_sem=gr.at[slot], device_id=core_dev, device_id_type=MESH,
        )

    def z_copy(idx, h, dev):
        return pltpu.make_async_remote_copy(
            src_ref=sbuf.at[idx, h], dst_ref=rbuf.at[idx, h], send_sem=zs.at[idx * CUT + h],
            recv_sem=zr.at[idx * CUT + h], device_id=dev, device_id_type=MESH,
        )

    loads[2].wait()
    loads[3].wait()

    @pl.loop(0, RING)
    def _(p):
        for g in range(FCOLS // G):
            cols = pl.ds(pl.multiple_of(p * FCOLS + g * G, G), G)
            grad = bv[:, cols] - lv[:, cols]
            top = jnp.max(jnp.abs(grad), axis=1, keepdims=True)
            scale = (top + SCALE_EPS).astype(BF16).astype(F32)
            level = (grad / scale).astype(BF16).astype(F32)
            vbuf[p, :, g * G : (g + 1) * G] = (level * scale).astype(BF16)

    words = [
        pick([packed((codes[n : n + 4] + (127,) * 3)[:4], 7) for codes in ORDER], row) for n in range(0, len(ORDER[0]), 4)
    ]
    arrival = pick([packed([u - 8 for u in parts], 3) for parts in ARRIVAL], row)

    loads[0].wait()
    loads[1].wait()

    @pl.loop(0, TOK // 128)
    def _(i):
        rows = pl.ds(pl.multiple_of(i * 128, 128), 128)
        xg[rows, :] = (tok[rows, :].astype(F32) * gvec[...].reshape(1, FEAT)).astype(BF16)

    for j in range(FIRST, 8):
        part_loads[j].wait()

    @pl.when(t >= RING // 2)
    def _():
        for copy in x_copies[FIRST:]:
            copy.start()

    told(group_sem, RING - 1 - k + 1 - xh)
    for delta in range(1, RING):
        rs_copy(delta).start()

    near = jnp.where(t == 0, 2, jnp.where(t == RING - 1, 0, 1))
    told(near_sem, near)

    def own_product(q):
        both = jnp.concatenate([wl[2 * q], wl[2 * q + 1]], axis=1)
        res = jnp.dot(xg[...], both, preferred_element_type=F32)
        prod[2 * q] = res[:, :128].reshape(CUT, PART, 128)
        prod[2 * q + 1] = res[:, 128:].reshape(CUT, PART, 128)

    def other_product(j):
        pltpu.make_async_remote_copy(
            src_ref=wr.at[j], dst_ref=wr.at[j], send_sem=xs.at[j], recv_sem=xrs.at[j],
            device_id=x_dev, device_id_type=MESH,
        ).wait_recv()
        u = 8 + lax.bitwise_and(lax.shift_right_logical(arrival, 3 * j), jnp.int32(7))

        prod[u] = jnp.dot(xg[...], wr[j], preferred_element_type=F32).reshape(CUT, PART, 128)

    def last_product(h):
        @pl.when(h == 0)
        def _():
            x_copies[7].wait_recv()

        u = 8 + lax.bitwise_and(lax.shift_right_logical(arrival, 21), jnp.int32(7))
        rows = pl.ds(pl.multiple_of(h * PART, PART), PART)
        prod[u, h] = jnp.dot(xg[rows, :], wr[7], preferred_element_type=F32)

    def pass_on(code):
        h = low(code, CUT)
        idx = lax.shift_right_logical(code, CUT.bit_length() - 1)
        up = lax.shift_right_logical(idx, 3)
        r = lax.shift_right_logical(low(idx, 8), 1) + 1
        s = low(idx, 2)
        step = 2 * up - 1
        u = 2 * low(place + step * r + RING, RING) + s
        dev = (rep, low(t + step + RING, RING), f)
        first = (r == 4) | ((r == 3) & (s == 1 - up))

        @pl.when(first)
        def _():
            sbuf[idx, h] = prod[u, h].astype(BF16)

        @pl.when(jnp.logical_not(first))
        def _():
            z_copy(idx + 2, h, dev).wait_recv()

            sbuf[idx, h] = (prod[u, h] + rbuf[idx + 2, h].astype(F32)).astype(BF16)

        z_copy(idx, h, dev).start()

    def squares():
        ones = jnp.ones((16, FEAT), BF16)
        sub = lax.broadcasted_iota(jnp.int32, (8, 128), 0)
        acc = jnp.zeros((8, 128), F32)
        for i in range(TOK // 256):
            x = tok[i * 256 : (i + 1) * 256, :].astype(F32)
            x2 = x * x
            hi = x2.astype(BF16)
            lo = (x2 - hi.astype(F32)).astype(BF16)
            dims = (((1,), (1,)), ((), ()))
            row = lax.dot_general(ones, hi, dims, preferred_element_type=F32)
            row = row + lax.dot_general(ones, lo, dims, preferred_element_type=F32)
            for g in range(2):
                acc = acc + jnp.where(sub == 2 * i + g, row[0:8, g * 128 : (g + 1) * 128], 0.0)
        sq[...] = acc
        told(far_sem, RING - 1 - t - near)
        for delta in range(1, RING):
            sq_copy(delta).start()

    def fragment_sum():
        for delta in range(1, RING):
            rs_copy(delta).wait_recv()
        total = vbuf[k].astype(F32)
        for delta in range(1, RING):
            total = total + frecv[delta - 1].astype(F32)
        fsum[...] = total.astype(BF16)
        h_copy().start()

        @pl.when(t < RING // 2)
        def _():
            for copy in x_copies[FIRST:]:
                copy.start()

    def fragment_spread():
        h_copy().wait_recv()
        fown[...] = (fsum[...].astype(F32) + xr[...].astype(F32)).astype(BF16)
        for delta in (2, 4, 6):
            ag_copy(delta).start()
        core_copy(0).start()

    def fragment_pass():
        for delta in (2, 4, 6):
            ag_copy(delta).wait_recv()
            core_copy(delta).start()

    def fragment_end():
        for delta in (1, 3, 5, 7):
            ag_copy(delta).wait_recv()
        loads[4].wait()

        for delta in range(RING):
            p = lax.rem(k + RING - delta, RING)
            cols = pl.ds(pl.multiple_of(p * FCOLS, FCOLS), FCOLS)
            piece = fown[...] if delta == 0 else fall[delta - 1]
            average = piece.astype(F32) / REPLICAS
            new_mom = OUTER_MOMENTUM * mv[:, cols] + average
            out_mom[:, cols] = new_mom
            out_base[:, cols] = bv[:, cols] - OUTER_RATE * (average + OUTER_MOMENTUM * new_mom)

    def row_scale():
        total = sq[...]
        for delta in range(1, RING):
            sq_copy(delta).wait_recv()
            total = total + sqr[delta - 1]
        rs = lax.rsqrt(total / WIDTH + NORM_EPS)
        for g in range(TOK // 128):
            rsf[g * 128 // PART, g * 128 % PART : g * 128 % PART + 128, :] = jnp.broadcast_to(rs[g : g + 1, :], (128, 128)).T

    def do(code):
        sends = (code >= 16) & (code < 16 + 16 * CUT)

        @pl.when(sends)
        def _():
            pass_on(code - 16)

        @pl.when(jnp.logical_not(sends))
        def _():
            @pl.when(code < 4)
            def _():
                own_product(code)

            @pl.when((code >= 8) & (code < 16))
            def _():
                other_product(code - 8)

            @pl.when(code == 4)
            def _():
                squares()

            @pl.when(code == 5)
            def _():
                fragment_sum()

            @pl.when(code == 6)
            def _():
                fragment_spread()

            @pl.when(code == 7)
            def _():
                fragment_end()

            @pl.when(code == 16 + 16 * CUT)
            def _():
                fragment_pass()

            @pl.when((code > 16 + 16 * CUT) & (code <= 16 + 17 * CUT))
            def _():
                last_product(code - (17 + 16 * CUT))

            @pl.when(code == 17 + 17 * CUT)
            def _():
                row_scale()

    @pl.loop(0, len(words))
    def _(n):
        word = words[0]
        for i in range(1, len(words)):
            word = jnp.where(n == i, words[i], word)

        @pl.loop(0, 4)
        def _(m):
            do(low(lax.shift_right_logical(word, 7 * m), 128))

    for h in range(CUT):
        for s in range(2):
            z_copy(s, h, on_ring(1)).wait_recv()
            z_copy(8 + s, h, on_ring(1)).wait_recv()

            total = prod[2 * place + s, h] + rbuf[s, h].astype(F32) + rbuf[8 + s, h].astype(F32)
            out[h * PART : (h + 1) * PART, s * 128 : (s + 1) * 128] = (total * rsf[h]).astype(BF16)

    for copy in x_copies:
        copy.wait_send()
    for idx in range(16):
        if idx in (6 + 1, 8 + 6):
            continue
        for h in range(CUT):
            z_copy(idx, h, on_ring(1)).wait_send()
    for delta in range(1, RING):
        sq_copy(delta).wait_send()
        rs_copy(delta).wait_send()
    for delta in (2, 4, 6):
        ag_copy(delta).wait_send()
        core_copy(delta).wait_send()
    core_copy(0).wait_send()
    h_copy().wait_send()


def write_out(a, b, c, a_out, b_out, c_out, sem):
    copies = []
    for src, dst in ((a, a_out), (b, b_out), (c, c_out)):
        rows = src.shape[0] // 2
        for i in range(2):
            part = pl.ds(i * rows, rows)
            copies.append(pltpu.make_async_copy(src.at[part], dst.at[part], sem.at[len(copies)]))
            copies[-1].start()
    for copy in copies:
        copy.wait()


def body(tokens, gain, weight, local, base, momentum):
    dma = pltpu.SemaphoreType.DMA
    any_spec = pl.BlockSpec(memory_space=pltpu.HBM)
    parts = pl.pallas_call(
        kernel,
        out_shape=(
            pltpu.VMEM((TOK, 256), BF16),
            pltpu.VMEM(base.shape, F32),
            pltpu.VMEM(base.shape, F32),
        ),
        in_specs=[any_spec] * 6,
        out_specs=[pl.BlockSpec(memory_space=pltpu.VMEM)] * 3,
        scratch_shapes=[
            pltpu.VMEM((TOK, FEAT), BF16),
            pltpu.VMEM((TOK, FEAT), BF16),
            pltpu.VMEM((FEAT,), F32),
            pltpu.VMEM((8, FEAT, 128), BF16),
            pltpu.VMEM((8, FEAT, 128), BF16),
            pltpu.VMEM((16, CUT, PART, 128), F32),
            pltpu.VMEM((16, CUT, PART, 128), BF16),
            pltpu.VMEM((16, CUT, PART, 128), BF16),
            pltpu.VMEM((8, 128), F32),
            pltpu.VMEM((RING - 1, 8, 128), F32),
            pltpu.VMEM((CUT, PART, 128), F32),
            pltpu.VMEM((FROWS, WIDTH), F32),
            pltpu.VMEM((FROWS, WIDTH), F32),
            pltpu.VMEM((FROWS, WIDTH), F32),
            pltpu.VMEM((RING, FROWS, FCOLS), BF16),
            pltpu.VMEM((RING - 1, FROWS, FCOLS), BF16),
            pltpu.VMEM((FROWS, FCOLS), BF16),
            pltpu.VMEM((FROWS, FCOLS), BF16),
            pltpu.VMEM((FROWS, FCOLS), BF16),
            pltpu.VMEM((RING - 1, FROWS, FCOLS), BF16),
            pltpu.SemaphoreType.REGULAR,
            pltpu.SemaphoreType.REGULAR,
            pltpu.SemaphoreType.REGULAR,
            dma((5 + 8,)),
            dma((8,)),
            dma((8,)),
            dma((16 * CUT,)),
            dma((16 * CUT,)),
            dma((RING - 1,)),
            dma((RING - 1,)),
            dma((RING - 1,)),
            dma((RING - 1,)),
            dma((1,)),
            dma((1,)),
            dma((RING - 1,)),
            dma((RING - 1,)),
        ],
        compiler_params=pltpu.CompilerParams(
            collective_id=0, has_side_effects=True, vmem_limit_bytes=50 * 1024 * 1024
        ),
    )(tokens, pltpu.with_memory_space_constraint(gain, pltpu.HBM), weight, local, base, momentum)
    return pl.pallas_call(
        write_out,
        out_shape=tuple(jax.ShapeDtypeStruct(part.shape, part.dtype) for part in parts),
        in_specs=[pl.BlockSpec(memory_space=pl.ANY)] * 3,
        out_specs=[any_spec] * 3,
        scratch_shapes=[dma((6,))],
        compiler_params=pltpu.CompilerParams(vmem_limit_bytes=1024 * 1024),
    )(*parts)


def solution(mesh):
    placed = (
        P(("replica", "fsdp"), "tensor"),
        P("tensor"),
        P("replica", "tensor", "fsdp"),
        P("replica", ("tensor", "fsdp"), None),
        P(("tensor", "fsdp"), None),
        P(("tensor", "fsdp"), None),
    )
    return jax.shard_map(
        body,
        mesh=mesh,
        in_specs=placed,
        out_specs=(
            P(("replica", "fsdp"), "tensor"),
            P(("tensor", "fsdp"), None),
            P(("tensor", "fsdp"), None),
        ),
        check_vma=False,
    )
```

```python
import jax
import jax.numpy as jnp
from jax import lax
from jax.experimental import pallas as pl
from jax.experimental.pallas import tpu as pltpu
from jax.sharding import PartitionSpec as P

F32 = jnp.float32
BF16 = jnp.bfloat16
MESH = pl.DeviceIdType.MESH

G = 128
OUTER_MOMENTUM = 0.9
OUTER_RATE = 0.7
NORM_EPS = 1e-05
SCALE_EPS = 1e-06
REPLICAS = 16
WIDTH = 8192
RING = 8
FIRST = 5
TOK = 1024
FEAT = 1024
COLS = 48
CUT = 4
PART = TOK // CUT
FROWS = 48
FCOLS = 1024

ORDER = (
    (
        2, 8, 0, 1, 3, 64, 65, 4, 9, 66, 67, 40, 41, 76, 42, 77, 43, 78, 10, 79, 36, 37, 85, 68,
        38, 69, 39, 5, 70, 11, 24, 25, 56, 71, 26, 60, 27, 61, 12, 62, 63, 52, 53, 6, 57, 58, 13, 59,
        32, 33, 54, 34, 80, 48, 35, 55, 7, 14, 28, 29, 30, 49, 31, 50, 81, 82, 83, 84, 20, 51, 21, 22,
        23, 16, 17, 18, 19,
    ),
    (
        2, 1, 3, 8, 0, 76, 77, 4, 78, 79, 9, 56, 32, 57, 33, 58, 34, 59, 35, 10, 68, 20, 85, 69,
        21, 70, 22, 5, 71, 23, 11, 60, 40, 41, 61, 42, 62, 43, 48, 12, 36, 37, 63, 52, 16, 53, 17, 54,
        6, 18, 55, 19, 38, 13, 64, 65, 39, 66, 80, 67, 49, 7, 14, 28, 29, 50, 51, 30, 31, 81, 82, 83,
        84, 24, 25, 26, 27,
    ),
    (
        1, 3, 2, 8, 0, 40, 41, 4, 42, 43, 9, 76, 77, 28, 78, 29, 79, 30, 48, 31, 10, 64, 85, 65,
        20, 66, 21, 5, 67, 22, 11, 68, 23, 69, 24, 70, 25, 71, 26, 12, 52, 27, 36, 53, 37, 54, 38, 49,
        6, 39, 55, 16, 50, 17, 13, 60, 18, 61, 19, 62, 80, 63, 7, 14, 32, 33, 51, 34, 35, 81, 82, 83,
        84, 56, 57, 58, 59,
    ),
    (
        3, 0, 2, 8, 1, 36, 37, 4, 38, 39, 9, 64, 65, 40, 66, 28, 67, 29, 30, 10, 31, 76, 77, 85,
        32, 78, 33, 79, 5, 34, 11, 35, 68, 69, 41, 70, 42, 71, 43, 12, 24, 56, 57, 25, 58, 26, 59, 27,
        6, 20, 21, 13, 16, 60, 61, 17, 62, 18, 80, 63, 19, 7, 14, 52, 53, 22, 23, 54, 55, 81, 82, 83,
        84, 48, 49, 50, 51,
    ),
    (
        2, 0, 3, 8, 1, 36, 37, 76, 77, 4, 38, 39, 78, 9, 40, 79, 41, 42, 43, 10, 64, 65, 32, 85,
        66, 33, 34, 67, 5, 35, 11, 68, 69, 28, 20, 70, 29, 71, 30, 12, 56, 57, 31, 24, 58, 25, 59, 26,
        48, 13, 27, 49, 21, 50, 22, 51, 16, 52, 17, 14, 53, 18, 60, 19, 54, 23, 55, 81, 82, 83, 84, 61,
        62, 63, 6, 80, 7,
    ),
    (
        0, 3, 2, 8, 1, 36, 37, 76, 77, 4, 38, 39, 78, 9, 79, 40, 64, 41, 65, 42, 66, 43, 67, 10,
        32, 68, 85, 28, 69, 33, 70, 5, 34, 71, 11, 35, 56, 24, 57, 25, 58, 26, 59, 12, 27, 29, 30, 16,
        48, 13, 49, 20, 21, 50, 22, 51, 31, 23, 14, 60, 61, 17, 62, 18, 63, 19, 81, 82, 83, 84, 52, 6,
        53, 54, 55, 80, 7,
    ),
    (
        0, 2, 1, 8, 3, 40, 41, 76, 77, 4, 42, 43, 78, 9, 79, 32, 68, 36, 69, 33, 70, 34, 71, 10,
        24, 64, 85, 35, 65, 25, 66, 5, 26, 67, 11, 27, 56, 37, 57, 38, 58, 28, 59, 12, 29, 60, 30, 61,
        31, 62, 39, 63, 13, 48, 49, 50, 51, 14, 16, 52, 17, 81, 82, 83, 84, 18, 53, 54, 20, 19, 55, 21,
        6, 22, 23, 80, 7,
    ),
    (
        3, 0, 2, 8, 1, 76, 77, 40, 41, 4, 78, 79, 42, 9, 43, 68, 32, 64, 33, 69, 34, 70, 35, 10,
        71, 85, 60, 61, 5, 62, 11, 36, 37, 63, 65, 38, 66, 39, 67, 16, 12, 48, 17, 56, 18, 49, 19, 50,
        28, 13, 51, 29, 57, 30, 58, 31, 59, 24, 52, 14, 25, 53, 26, 54, 27, 55, 20, 21, 81, 82, 83, 84,
        22, 23, 6, 80, 7,
    ),
    (
        2, 0, 3, 8, 1, 40, 41, 64, 65, 4, 42, 43, 66, 9, 67, 56, 57, 48, 32, 49, 10, 85, 50, 33,
        34, 51, 35, 58, 5, 68, 11, 36, 69, 37, 38, 70, 39, 71, 52, 12, 28, 29, 53, 54, 30, 59, 31, 24,
        13, 25, 76, 77, 26, 78, 27, 79, 14, 55, 16, 60, 17, 61, 81, 82, 18, 83, 84, 62, 19, 63, 20, 6,
        21, 22, 23, 80, 7,
    ),
    (
        2, 1, 3, 8, 0, 76, 77, 4, 78, 79, 9, 40, 56, 41, 42, 57, 43, 58, 16, 59, 10, 64, 17, 85,
        20, 65, 18, 66, 5, 19, 67, 11, 36, 48, 37, 49, 38, 50, 39, 60, 12, 32, 61, 33, 62, 34, 63, 35,
        21, 13, 22, 23, 51, 24, 14, 25, 68, 69, 26, 70, 27, 71, 81, 28, 82, 29, 83, 30, 84, 52, 31, 53,
        6, 54, 55, 80, 7,
    ),
    (
        1, 0, 2, 8, 3, 76, 77, 4, 78, 79, 9, 64, 24, 65, 25, 66, 28, 67, 26, 10, 48, 27, 85, 49,
        50, 5, 51, 11, 40, 41, 68, 69, 42, 70, 43, 71, 29, 12, 56, 30, 57, 31, 58, 16, 59, 13, 32, 33,
        52, 53, 34, 54, 35, 55, 14, 36, 37, 38, 39, 17, 81, 60, 82, 61, 83, 84, 62, 18, 19, 63, 20, 6,
        21, 22, 23, 80, 7,
    ),
    (
        0, 2, 3, 8, 1, 64, 65, 32, 4, 66, 33, 67, 36, 9, 68, 34, 35, 69, 20, 70, 21, 71, 10, 22,
        85, 23, 76, 77, 24, 78, 5, 37, 79, 11, 38, 56, 39, 57, 58, 59, 12, 40, 41, 42, 43, 16, 13, 17,
        60, 61, 18, 62, 19, 63, 25, 14, 48, 49, 26, 27, 50, 28, 51, 29, 81, 82, 83, 84, 30, 31, 52, 6,
        53, 54, 55, 80, 7,
    ),
    (
        2, 8, 0, 3, 1, 40, 41, 4, 9, 42, 43, 76, 77, 28, 78, 29, 79, 30, 10, 64, 31, 65, 85, 32,
        66, 20, 67, 5, 21, 11, 56, 57, 22, 23, 58, 16, 59, 17, 68, 12, 18, 69, 19, 70, 24, 71, 25, 6,
        48, 26, 49, 27, 50, 13, 33, 60, 34, 61, 80, 35, 62, 36, 63, 7, 14, 52, 37, 38, 51, 39, 53, 54,
        81, 82, 83, 84, 55,
    ),
    (
        2, 3, 1, 8, 0, 64, 65, 36, 37, 4, 66, 67, 38, 9, 76, 39, 40, 77, 28, 78, 29, 79, 30, 10,
        68, 31, 85, 69, 24, 70, 25, 5, 71, 26, 11, 56, 27, 57, 32, 58, 33, 59, 34, 12, 48, 35, 49, 41,
        50, 42, 51, 6, 43, 60, 61, 13, 62, 20, 21, 63, 22, 80, 23, 52, 7, 14, 53, 54, 55, 81, 82, 83,
        84, 16, 17, 18, 19,
    ),
    (
        2, 0, 1, 8, 3, 36, 37, 64, 65, 4, 38, 39, 66, 9, 32, 67, 76, 33, 77, 34, 78, 35, 68, 10,
        85, 69, 40, 41, 70, 42, 71, 5, 43, 79, 11, 24, 60, 25, 61, 26, 62, 27, 63, 12, 28, 56, 29, 57,
        30, 58, 31, 6, 59, 20, 21, 13, 22, 23, 52, 16, 53, 80, 17, 54, 7, 14, 55, 48, 18, 19, 49, 50,
        81, 82, 83, 84, 51,
    ),
    (
        3, 0, 2, 8, 40, 41, 1, 42, 64, 65, 4, 43, 66, 9, 36, 56, 37, 57, 38, 58, 39, 59, 32, 10,
        67, 85, 76, 33, 34, 77, 35, 78, 5, 79, 11, 24, 60, 25, 61, 26, 62, 27, 52, 12, 28, 53, 29, 54,
        30, 55, 31, 6, 48, 20, 49, 21, 50, 13, 22, 51, 23, 63, 80, 16, 68, 17, 69, 7, 14, 18, 19, 70,
        71, 81, 82, 83, 84,
    ),
)
ARRIVAL = (
    (
        9, 8, 11, 12, 15, 10, 13, 14,
    ),
    (
        11, 12, 9, 10, 13, 8, 15, 14,
    ),
    (
        12, 13, 10, 11, 15, 9, 14, 8,
    ),
    (
        14, 12, 15, 13, 10, 11, 9, 8,
    ),
    (
        11, 10, 14, 15, 12, 9, 13, 8,
    ),
    (
        13, 10, 14, 12, 8, 9, 15, 11,
    ),
    (
        8, 9, 12, 14, 15, 10, 13, 11,
    ),
    (
        13, 8, 12, 9, 11, 10, 14, 15,
    ),
    (
        8, 10, 12, 11, 13, 9, 14, 15,
    ),
    (
        11, 10, 8, 13, 12, 14, 9, 15,
    ),
    (
        13, 10, 11, 12, 8, 14, 15, 9,
    ),
    (
        12, 13, 15, 10, 14, 11, 8, 9,
    ),
    (
        11, 15, 14, 12, 10, 13, 8, 9,
    ),
    (
        13, 14, 10, 15, 12, 9, 11, 8,
    ),
    (
        11, 8, 15, 13, 9, 10, 14, 12,
    ),
    (
        8, 9, 13, 10, 11, 12, 14, 15,
    ),
)


def pick(values, row):
    value = jnp.int32(values[0])
    for c in range(1, len(values)):
        value = jnp.where(row == c, jnp.int32(values[c]), value)
    return value


def low(value, size):
    return lax.bitwise_and(value, jnp.int32(size - 1))


def packed(codes, bits):
    return sum(code << (bits * i) for i, code in enumerate(codes))


def kernel(
    tokens, gain, weight, local, base, momentum,
    out, out_base, out_mom,
    tok, xg, gvec, wl, wr, prod, sbuf, rbuf, sq, sqr, rsf,
    bv, lv, mv, vbuf, frecv, fsum, xr, fown, fall,
    near_sem, far_sem, group_sem, load_sem, xs, xrs, zs, zr, qs, qr, fs, fr, hs, hr, gs, gr,
):
    rep = lax.axis_index("replica")
    t = lax.axis_index("tensor")
    f = lax.axis_index("fsdp")
    place = lax.rem(t + 4 * f, RING)
    row = f * RING + place
    other = (1 - f) * RING + lax.rem(place + 4, RING)
    y = rep // 4
    xh = lax.rem(rep // 2, 2)
    core = lax.rem(rep, 2)
    k = y * 2 + core

    def member(delta):
        p = lax.rem(k + delta, RING)
        return p, ((p // 2) * 4 + xh * 2 + lax.rem(p, 2), t, f)

    def on_ring(delta):
        return (rep, lax.rem(t + delta, RING), f)

    x_dev = (rep, t, 1 - f)
    h_dev = (y * 4 + (1 - xh) * 2 + core, t, f)

    def told(sem, count):
        @pl.when(count > 0)
        def _():
            pl.semaphore_wait(sem, count)

    barrier = pltpu.get_barrier_semaphore()
    pl.semaphore_signal(barrier, inc=1, device_id=x_dev, device_id_type=MESH)

    parts = [pick([codes[j] - 8 for codes in ARRIVAL], other) for j in range(8)]
    part_loads = [
        pltpu.make_async_copy(
            weight.at[0, :, pl.ds(pl.multiple_of(parts[j] * 128, 128), 128)], wl.at[parts[j]], load_sem.at[5 + j]
        )
        for j in range(8)
    ]
    for j in range(FIRST):
        part_loads[j].start()

    def on_pair(mine, theirs, sem, dev):
        @pl.when(mine < theirs if sem is barrier else mine > theirs)
        def _():
            pl.semaphore_signal(sem, inc=1, device_id=dev, device_id_type=MESH)

    def tell(near, far, group):
        for delta in range(1, RING):
            sem = near if delta in (1, RING - 1) else far
            on_pair(t, lax.rem(t + delta, RING), sem, on_ring(delta))
        for delta in range(1, RING):
            p, dev = member(delta)
            on_pair(k, p, group, dev)
        on_pair(xh, 1 - xh, group, h_dev)

    tell(barrier, barrier, barrier)
    loads = [
        pltpu.make_async_copy(src, dst, load_sem.at[i])
        for i, (src, dst) in enumerate(
            ((tokens, tok), (gain, gvec), (base, bv), (local.at[0], lv), (momentum, mv))
        )
    ]
    pl.semaphore_wait(barrier, 1 + t + k + xh)

    x_copies = []
    for j in range(8):
        x_copies.append(
            pltpu.make_async_remote_copy(
                src_ref=wl.at[parts[j]],
                dst_ref=wr.at[j],
                send_sem=xs.at[j],
                recv_sem=xrs.at[j],
                device_id=x_dev,
                device_id_type=MESH,
            )
        )
    for j in range(FIRST):
        part_loads[j].wait()
        x_copies[j].start()
    for load in loads + part_loads[FIRST:]:
        load.start()

    tell(near_sem, far_sem, group_sem)

    def sq_copy(delta):
        return pltpu.make_async_remote_copy(
            src_ref=sq, dst_ref=sqr.at[delta - 1], send_sem=qs.at[delta - 1], recv_sem=qr.at[delta - 1],
            device_id=on_ring(delta), device_id_type=MESH,
        )

    def rs_copy(delta):
        p, dev = member(delta)
        return pltpu.make_async_remote_copy(
            src_ref=vbuf.at[p], dst_ref=frecv.at[delta - 1], send_sem=fs.at[delta - 1],
            recv_sem=fr.at[delta - 1], device_id=dev, device_id_type=MESH,
        )

    def h_copy():
        return pltpu.make_async_remote_copy(
            src_ref=fsum, dst_ref=xr, send_sem=hs.at[0], recv_sem=hr.at[0], device_id=h_dev, device_id_type=MESH
        )

    core_dev = (y * 4 + xh * 2 + 1 - core, t, f)
    step_core = 1 - 2 * core

    def ag_copy(delta):
        return pltpu.make_async_remote_copy(
            src_ref=fown, dst_ref=fall.at[delta - 1], send_sem=gs.at[delta - 1], recv_sem=gr.at[delta - 1],
            device_id=member(delta)[1], device_id_type=MESH,
        )

    def core_copy(delta):
        slot = lax.rem(delta + step_core + RING, RING) - 1
        return pltpu.make_async_remote_copy(
            src_ref=fall.at[delta - 1] if delta else fown, dst_ref=fall.at[slot], send_sem=gs.at[delta],
            recv_sem=gr.at[slot], device_id=core_dev, device_id_type=MESH,
        )

    def z_copy(idx, h, dev):
        return pltpu.make_async_remote_copy(
            src_ref=sbuf.at[idx, h], dst_ref=rbuf.at[idx, h], send_sem=zs.at[idx * CUT + h],
            recv_sem=zr.at[idx * CUT + h], device_id=dev, device_id_type=MESH,
        )

    loads[2].wait()
    loads[3].wait()

    @pl.loop(0, RING)
    def _(p):
        for g in range(FCOLS // G):
            cols = pl.ds(pl.multiple_of(p * FCOLS + g * G, G), G)
            grad = bv[:, cols] - lv[:, cols]
            top = jnp.max(jnp.abs(grad), axis=1, keepdims=True)
            scale = (top + SCALE_EPS).astype(BF16).astype(F32)
            level = (grad / scale).astype(BF16).astype(F32)
            vbuf[p, :, g * G : (g + 1) * G] = (level * scale).astype(BF16)

    words = [
        pick([packed((codes[n : n + 4] + (127,) * 3)[:4], 7) for codes in ORDER], row) for n in range(0, len(ORDER[0]), 4)
    ]
    arrival = pick([packed([u - 8 for u in parts], 3) for parts in ARRIVAL], row)

    loads[0].wait()
    loads[1].wait()

    @pl.loop(0, TOK // 128)
    def _(i):
        rows = pl.ds(pl.multiple_of(i * 128, 128), 128)
        xg[rows, :] = (tok[rows, :].astype(F32) * gvec[...].reshape(1, FEAT)).astype(BF16)

    for j in range(FIRST, 8):
        part_loads[j].wait()

    @pl.when(t >= RING // 2)
    def _():
        for copy in x_copies[FIRST:]:
            copy.start()

    told(group_sem, RING - 1 - k + 1 - xh)
    for delta in range(1, RING):
        rs_copy(delta).start()

    near = jnp.where(t == 0, 2, jnp.where(t == RING - 1, 0, 1))
    told(near_sem, near)

    def own_product(q):
        both = jnp.concatenate([wl[2 * q], wl[2 * q + 1]], axis=1)
        res = jnp.dot(xg[...], both, preferred_element_type=F32)
        prod[2 * q] = res[:, :128].reshape(CUT, PART, 128)
        prod[2 * q + 1] = res[:, 128:].reshape(CUT, PART, 128)

    def other_product(j):
        pltpu.make_async_remote_copy(
            src_ref=wr.at[j], dst_ref=wr.at[j], send_sem=xs.at[j], recv_sem=xrs.at[j],
            device_id=x_dev, device_id_type=MESH,
        ).wait_recv()
        u = 8 + lax.bitwise_and(lax.shift_right_logical(arrival, 3 * j), jnp.int32(7))

        prod[u] = jnp.dot(xg[...], wr[j], preferred_element_type=F32).reshape(CUT, PART, 128)

    def last_product(h):
        @pl.when(h == 0)
        def _():
            x_copies[7].wait_recv()

        u = 8 + lax.bitwise_and(lax.shift_right_logical(arrival, 21), jnp.int32(7))
        rows = pl.ds(pl.multiple_of(h * PART, PART), PART)
        prod[u, h] = jnp.dot(xg[rows, :], wr[7], preferred_element_type=F32)

    def pass_on(code):
        h = low(code, CUT)
        idx = lax.shift_right_logical(code, CUT.bit_length() - 1)
        up = lax.shift_right_logical(idx, 3)
        r = lax.shift_right_logical(low(idx, 8), 1) + 1
        s = low(idx, 2)
        step = 2 * up - 1
        u = 2 * low(place + step * r + RING, RING) + s
        dev = (rep, low(t + step + RING, RING), f)
        first = (r == 4) | ((r == 3) & (s == 1 - up))

        @pl.when(first)
        def _():
            sbuf[idx, h] = prod[u, h].astype(BF16)

        @pl.when(jnp.logical_not(first))
        def _():
            z_copy(idx + 2, h, dev).wait_recv()

            sbuf[idx, h] = (prod[u, h] + rbuf[idx + 2, h].astype(F32)).astype(BF16)

        z_copy(idx, h, dev).start()

    def squares():
        ones = jnp.ones((16, FEAT), BF16)
        sub = lax.broadcasted_iota(jnp.int32, (8, 128), 0)
        acc = jnp.zeros((8, 128), F32)
        for i in range(TOK // 256):
            x = tok[i * 256 : (i + 1) * 256, :].astype(F32)
            x2 = x * x
            hi = x2.astype(BF16)
            lo = (x2 - hi.astype(F32)).astype(BF16)
            dims = (((1,), (1,)), ((), ()))
            row = lax.dot_general(ones, hi, dims, preferred_element_type=F32)
            row = row + lax.dot_general(ones, lo, dims, preferred_element_type=F32)
            for g in range(2):
                acc = acc + jnp.where(sub == 2 * i + g, row[0:8, g * 128 : (g + 1) * 128], 0.0)
        sq[...] = acc
        told(far_sem, RING - 1 - t - near)
        for delta in range(1, RING):
            sq_copy(delta).start()

    def fragment_sum():
        for delta in range(1, RING):
            rs_copy(delta).wait_recv()
        total = vbuf[k].astype(F32)
        for delta in range(1, RING):
            total = total + frecv[delta - 1].astype(F32)
        fsum[...] = total.astype(BF16)
        h_copy().start()

        @pl.when(t < RING // 2)
        def _():
            for copy in x_copies[FIRST:]:
                copy.start()

    def fragment_spread():
        h_copy().wait_recv()
        fown[...] = (fsum[...].astype(F32) + xr[...].astype(F32)).astype(BF16)
        for delta in (2, 4, 6):
            ag_copy(delta).start()
        core_copy(0).start()

    def fragment_pass():
        for delta in (2, 4, 6):
            ag_copy(delta).wait_recv()
            core_copy(delta).start()

    def fragment_end():
        for delta in (1, 3, 5, 7):
            ag_copy(delta).wait_recv()
        loads[4].wait()

        for delta in range(RING):
            p = lax.rem(k + RING - delta, RING)
            cols = pl.ds(pl.multiple_of(p * FCOLS, FCOLS), FCOLS)
            piece = fown[...] if delta == 0 else fall[delta - 1]
            average = piece.astype(F32) / REPLICAS
            new_mom = OUTER_MOMENTUM * mv[:, cols] + average
            out_mom[:, cols] = new_mom
            out_base[:, cols] = bv[:, cols] - OUTER_RATE * (average + OUTER_MOMENTUM * new_mom)

    def row_scale():
        total = sq[...]
        for delta in range(1, RING):
            sq_copy(delta).wait_recv()
            total = total + sqr[delta - 1]
        rs = lax.rsqrt(total / WIDTH + NORM_EPS)
        for g in range(TOK // 128):
            rsf[g * 128 // PART, g * 128 % PART : g * 128 % PART + 128, :] = jnp.broadcast_to(rs[g : g + 1, :], (128, 128)).T

    def do(code):
        sends = (code >= 16) & (code < 16 + 16 * CUT)

        @pl.when(sends)
        def _():
            pass_on(code - 16)

        @pl.when(jnp.logical_not(sends))
        def _():
            @pl.when(code < 4)
            def _():
                own_product(code)

            @pl.when((code >= 8) & (code < 16))
            def _():
                other_product(code - 8)

            @pl.when(code == 4)
            def _():
                squares()

            @pl.when(code == 5)
            def _():
                fragment_sum()

            @pl.when(code == 6)
            def _():
                fragment_spread()

            @pl.when(code == 7)
            def _():
                fragment_end()

            @pl.when(code == 16 + 16 * CUT)
            def _():
                fragment_pass()

            @pl.when((code > 16 + 16 * CUT) & (code <= 16 + 17 * CUT))
            def _():
                last_product(code - (17 + 16 * CUT))

            @pl.when(code == 17 + 17 * CUT)
            def _():
                row_scale()

    @pl.loop(0, len(words))
    def _(n):
        word = words[0]
        for i in range(1, len(words)):
            word = jnp.where(n == i, words[i], word)

        @pl.loop(0, 4)
        def _(m):
            do(low(lax.shift_right_logical(word, 7 * m), 128))

    for h in range(CUT):
        for s in range(2):
            z_copy(s, h, on_ring(1)).wait_recv()
            z_copy(8 + s, h, on_ring(1)).wait_recv()

            total = prod[2 * place + s, h] + rbuf[s, h].astype(F32) + rbuf[8 + s, h].astype(F32)
            out[h * PART : (h + 1) * PART, s * 128 : (s + 1) * 128] = (total * rsf[h]).astype(BF16)

    for copy in x_copies:
        copy.wait_send()
    for idx in range(16):
        if idx in (6 + 1, 8 + 6):
            continue
        for h in range(CUT):
            z_copy(idx, h, on_ring(1)).wait_send()
    for delta in range(1, RING):
        sq_copy(delta).wait_send()
        rs_copy(delta).wait_send()
    for delta in (2, 4, 6):
        ag_copy(delta).wait_send()
        core_copy(delta).wait_send()
    core_copy(0).wait_send()
    h_copy().wait_send()


def write_out(a, b, c, a_out, b_out, c_out, sem):
    copies = []
    for src, dst in ((a, a_out), (b, b_out), (c, c_out)):
        rows = src.shape[0] // 2
        for i in range(2):
            part = pl.ds(i * rows, rows)
            copies.append(pltpu.make_async_copy(src.at[part], dst.at[part], sem.at[len(copies)]))
            copies[-1].start()
    for copy in copies:
        copy.wait()


def body(tokens, gain, weight, local, base, momentum):
    dma = pltpu.SemaphoreType.DMA
    any_spec = pl.BlockSpec(memory_space=pltpu.HBM)
    parts = pl.pallas_call(
        kernel,
        out_shape=(
            pltpu.VMEM((TOK, 256), BF16),
            pltpu.VMEM(base.shape, F32),
            pltpu.VMEM(base.shape, F32),
        ),
        in_specs=[any_spec] * 6,
        out_specs=[pl.BlockSpec(memory_space=pltpu.VMEM)] * 3,
        scratch_shapes=[
            pltpu.VMEM((TOK, FEAT), BF16),
            pltpu.VMEM((TOK, FEAT), BF16),
            pltpu.VMEM((FEAT,), F32),
            pltpu.VMEM((8, FEAT, 128), BF16),
            pltpu.VMEM((8, FEAT, 128), BF16),
            pltpu.VMEM((16, CUT, PART, 128), F32),
            pltpu.VMEM((16, CUT, PART, 128), BF16),
            pltpu.VMEM((16, CUT, PART, 128), BF16),
            pltpu.VMEM((8, 128), F32),
            pltpu.VMEM((RING - 1, 8, 128), F32),
            pltpu.VMEM((CUT, PART, 128), F32),
            pltpu.VMEM((FROWS, WIDTH), F32),
            pltpu.VMEM((FROWS, WIDTH), F32),
            pltpu.VMEM((FROWS, WIDTH), F32),
            pltpu.VMEM((RING, FROWS, FCOLS), BF16),
            pltpu.VMEM((RING - 1, FROWS, FCOLS), BF16),
            pltpu.VMEM((FROWS, FCOLS), BF16),
            pltpu.VMEM((FROWS, FCOLS), BF16),
            pltpu.VMEM((FROWS, FCOLS), BF16),
            pltpu.VMEM((RING - 1, FROWS, FCOLS), BF16),
            pltpu.SemaphoreType.REGULAR,
            pltpu.SemaphoreType.REGULAR,
            pltpu.SemaphoreType.REGULAR,
            dma((5 + 8,)),
            dma((8,)),
            dma((8,)),
            dma((16 * CUT,)),
            dma((16 * CUT,)),
            dma((RING - 1,)),
            dma((RING - 1,)),
            dma((RING - 1,)),
            dma((RING - 1,)),
            dma((1,)),
            dma((1,)),
            dma((RING - 1,)),
            dma((RING - 1,)),
        ],
        compiler_params=pltpu.CompilerParams(
            collective_id=0, has_side_effects=True, vmem_limit_bytes=50 * 1024 * 1024
        ),
    )(tokens, pltpu.with_memory_space_constraint(gain, pltpu.HBM), weight, local, base, momentum)
    return pl.pallas_call(
        write_out,
        out_shape=tuple(jax.ShapeDtypeStruct(part.shape, part.dtype) for part in parts),
        in_specs=[pl.BlockSpec(memory_space=pl.ANY)] * 3,
        out_specs=[any_spec] * 3,
        scratch_shapes=[dma((6,))],
        compiler_params=pltpu.CompilerParams(vmem_limit_bytes=1024 * 1024),
    )(*parts)


def solution(mesh):
    placed = (
        P(("replica", "fsdp"), "tensor"),
        P("tensor"),
        P("replica", "tensor", "fsdp"),
        P("replica", ("tensor", "fsdp"), None),
        P(("tensor", "fsdp"), None),
        P(("tensor", "fsdp"), None),
    )
    return jax.shard_map(
        body,
        mesh=mesh,
        in_specs=placed,
        out_specs=(
            P(("replica", "fsdp"), "tensor"),
            P(("tensor", "fsdp"), None),
            P(("tensor", "fsdp"), None),
        ),
        check_vma=False,
    )
```
